128 devices in a mesh: row: 16 (over x_hi, y, core), col: 8 (over z, x_lo).
Axes of the slice: x: 4 (x_hi: 2, x_lo: 2; x = x_hi * 2 + x_lo), y: 4, z: 4, core: 2. Of those that a mesh axis runs over, the one named last changes fastest.
Arguments:
- block_input: bfloat16 [512, 512, 256], P('row', 'col'), may hold values from -6 to 6
- cotangent: bfloat16 [512, 512, 256], P('row', 'col'), may hold values from -6 to 6
- conv_gain: float32 [256], replicated, may hold values from 0.25 to 1.75
- grid_gain: float32 [256], replicated, may hold values from 0.25 to 1.75
- mlp_gain: float32 [256], replicated, may hold values from 0.25 to 1.75
- expand_weight: bfloat16 [256, 1024], replicated, may hold values from -0.375 to 0.375
- depth_kernel: bfloat16 [3, 3, 1024], replicated, may hold values from -2 to 2
- shrink_weight: bfloat16 [1024, 256], replicated, may hold values from -0.1875 to 0.1875
- qkv_weight: bfloat16 [256, 768], replicated, may hold values from -0.375 to 0.375
- mix_weight: bfloat16 [256, 256], replicated, may hold values from -0.375 to 0.375
- grid_bias: float32 [8, 64, 64], replicated, may hold values from -3 to 320
- widen_weight: bfloat16 [256, 1024], replicated, may hold values from -0.375 to 0.375
- narrow_weight: bfloat16 [1024, 256], replicated, may hold values from -0.1875 to 0.1875
Outputs:
- block_out: bfloat16 [512, 512, 256], P('row', 'col')
- input_grad: bfloat16 [512, 512, 256], P('row', 'col')
- qkv_grad: float32 [256, 768], replicated
- mix_grad: float32 [256, 256], replicated
The draws below stay inside these ranges and needn't reach their ends.
All inputs are finite; a program needn't handle non-finite values.
Results may differ from the reference program's by a relative error of at most 0.017.
Values may be sent and summed in bfloat16 or wider, within the bound.
A program may use at most 192 MiB of HBM per device.

```python
import math
import jax
import jax.numpy as jnp
from jax import lax

D = 256
HEADS = 8
FF = 1024
FM = 1024
GRID = 8
HEIGHT = 512
WIDTH = 512


def draw_block_input(key, part):
    key = jax.random.fold_in(key, 7)
    subkeys = jax.random.split(key, 3)
    baseline = jnp.clip(jax.random.normal(subkeys[0], (HEIGHT, WIDTH, D), jnp.float32), -3.0, 3.0)
    row_scale = jnp.exp(jax.random.uniform(subkeys[1], (HEIGHT, WIDTH, 1), jnp.float32, -0.6, 0.6))
    col_scale = jnp.exp(jax.random.uniform(subkeys[2], (D,), jnp.float32, -0.6, 0.6))
    values = baseline * row_scale * col_scale
    return jnp.clip(values, -6.0, 6.0).astype(jnp.bfloat16)


def draw_grid_bias(key, part):
    key = jax.random.fold_in(key, 29)
    subkeys = jax.random.split(key, 1)
    members = GRID * GRID
    values = jnp.clip(jax.random.normal(subkeys[0], (HEADS, members, members), jnp.float32), -3.0, 3.0)
    return values.astype(jnp.float32)


def levels(stream_key, dims, pieces, low, top_value):
    level, own = 1.0, jax.random.fold_in(stream_key, 6)
    for dim, parts in pieces:
        steps = jnp.exp(jax.random.uniform(jax.random.fold_in(own, dim), (parts,), jnp.float32, low / len(pieces), top_value / len(pieces)))
        level = level * jnp.repeat(steps, dims[dim] // parts).reshape([-1 if axis == dim else 1 for axis in range(len(dims))])
    return level


def normal_values(own_key, shape, width, reach, shards=(), held_as=jnp.bfloat16):
    values = width * jax.random.normal(own_key, shape, jnp.float32)
    if shards:
        values = values * levels(own_key, shape, shards, -0.22, 0.18)
    return jnp.clip(values, -reach, reach).astype(held_as)


def setup_inputs(seed: int = 0) -> dict:
    key_list = jax.random.split(jax.random.key(seed), 14)
    block_input = draw_block_input(jax.random.fold_in(key_list[13], 71), 0)
    cotangent = normal_values(key_list[1], (HEIGHT, WIDTH, D), 1.0, 6.0, ((0, 16), (1, 8)))
    conv_gain = jnp.clip(1.0 + 0.15 * jax.random.normal(key_list[2], (D,), jnp.float32), 0.25, 1.75)
    grid_gain = jnp.clip(1.0 + 0.15 * jax.random.normal(key_list[3], (D,), jnp.float32), 0.25, 1.75)
    mlp_gain = jnp.clip(1.0 + 0.15 * jax.random.normal(key_list[4], (D,), jnp.float32), 0.25, 1.75)
    expand_weight = normal_values(key_list[5], (D, FF), D ** -0.5, 0.375)
    depth_kernel = normal_values(key_list[6], (3, 3, FF), 9 ** -0.5, 2.0)
    shrink_weight = normal_values(key_list[7], (FF, D), FF ** -0.5, 0.1875)
    qkv_weight = normal_values(key_list[8], (D, 3 * D), D ** -0.5, 0.375)
    mix_weight = normal_values(key_list[9], (D, D), D ** -0.5, 0.375)
    grid_bias = draw_grid_bias(jax.random.fold_in(key_list[13], 71), 0)
    widen_weight = normal_values(key_list[11], (D, FM), D ** -0.5, 0.375)
    narrow_weight = normal_values(key_list[12], (FM, D), FM ** -0.5, 0.1875)
    return dict(block_input=block_input, cotangent=cotangent, conv_gain=conv_gain, grid_gain=grid_gain, mlp_gain=mlp_gain, expand_weight=expand_weight, depth_kernel=depth_kernel, shrink_weight=shrink_weight, qkv_weight=qkv_weight, mix_weight=mix_weight, grid_bias=grid_bias, widen_weight=widen_weight, narrow_weight=narrow_weight)


def rounded(values):
    return lax.optimization_barrier(values.astype(jnp.bfloat16))

def gelu_tanh(inputs):
    inner = 0.7978845608028654 * (inputs + 0.044715 * inputs * inputs * inputs)
    return 0.5 * inputs * (1.0 + jnp.tanh(inner))

def gelu_slope(inputs):
    inner = 0.7978845608028654 * (inputs + 0.044715 * inputs * inputs * inputs)
    tangent = jnp.tanh(inner)
    return 0.5 * (1.0 + tangent) + 0.5 * inputs * (1.0 - tangent * tangent) * 0.7978845608028654 * (1.0 + 3.0 * 0.044715 * inputs * inputs)

def layer_norm(values, gain):
    widened = values.astype(jnp.float32)
    centre = widened - lax.optimization_barrier(jnp.mean(widened, axis=-1, keepdims=True))
    inv_std = lax.rsqrt(lax.optimization_barrier(jnp.mean(centre * centre, axis=-1, keepdims=True)) + 1e-05)
    return rounded(centre * inv_std * gain)

def norm_back(cotan, values, gain):
    widened = values.astype(jnp.float32)
    centre = widened - lax.optimization_barrier(jnp.mean(widened, axis=-1, keepdims=True))
    inv_std = lax.rsqrt(lax.optimization_barrier(jnp.mean(centre * centre, axis=-1, keepdims=True)) + 1e-05)
    normal = centre * inv_std
    scaled = cotan.astype(jnp.float32) * gain
    return inv_std * (scaled - lax.optimization_barrier(jnp.mean(scaled, axis=-1, keepdims=True)) - normal * lax.optimization_barrier(jnp.mean(scaled * normal, axis=-1, keepdims=True)))

def dense_product(left, right):
    return jnp.dot(left, right, preferred_element_type=jnp.float32)

def dense_transposed(left, right):
    return lax.dot_general(left, right, (((left.ndim - 1,), (1,)), ((), ())), preferred_element_type=jnp.float32)

def outer_sum(left, right):
    flat_left = left.reshape(-1, left.shape[-1])
    flat_right = right.reshape(-1, right.shape[-1])
    return lax.dot_general(flat_left, flat_right, (((0,), (0,)), ((), ())), preferred_element_type=jnp.float32)

def depthwise(padded, kernel):
    out_rows = padded.shape[0] - 2
    out_cols = padded.shape[1] - 2
    running = jnp.zeros((out_rows, out_cols, padded.shape[2]), jnp.float32)
    for shift_row in range(3):
        for shift_col in range(3):
            window = padded[shift_row:shift_row + out_rows, shift_col:shift_col + out_cols].astype(jnp.float32)
            running = running + window * kernel[shift_row, shift_col].astype(jnp.float32)
    return running

def depth_back(padded, kernel):
    out_rows = padded.shape[0] - 2
    out_cols = padded.shape[1] - 2
    running = jnp.zeros((out_rows, out_cols, padded.shape[2]), jnp.float32)
    for shift_row in range(3):
        for shift_col in range(3):
            window = padded[2 - shift_row:2 - shift_row + out_rows, 2 - shift_col:2 - shift_col + out_cols].astype(jnp.float32)
            running = running + window * kernel[shift_row, shift_col].astype(jnp.float32)
    return running

def attend(normed_sets, qkv_weight, mix_weight, grid_bias):
    set_count, members, channels = normed_sets.shape
    head_dim = channels // HEADS
    qkv_sets = rounded(dense_product(normed_sets, qkv_weight))
    heads_split = qkv_sets.reshape(set_count, members, 3, HEADS, head_dim).astype(jnp.float32)
    queries = heads_split[:, :, 0]
    key_heads = heads_split[:, :, 1]
    values = heads_split[:, :, 2]
    scores = jnp.einsum('smhd,snhd->shmn', queries, key_heads) / math.sqrt(head_dim) + grid_bias[None]
    row_max = lax.optimization_barrier(jnp.max(scores, axis=-1, keepdims=True))
    exponent = jnp.exp(scores - row_max)
    softmax_weights = exponent / lax.optimization_barrier(jnp.sum(exponent, axis=-1, keepdims=True))
    low_weights = rounded(softmax_weights).astype(jnp.float32)
    mixed = rounded(jnp.einsum('shmn,snhd->smhd', low_weights, values).reshape(set_count, members, channels))
    projected = rounded(dense_product(mixed, mix_weight))
    return (qkv_sets, softmax_weights, mixed, projected)

def attend_back(normed_sets, qkv_sets, softmax_weights, mixed, grad_sets, qkv_weight, mix_weight):
    set_count, members, channels = normed_sets.shape
    head_dim = channels // HEADS
    mix_part = outer_sum(mixed, grad_sets)
    mixed_grad = rounded(dense_transposed(grad_sets, mix_weight)).reshape(set_count, members, HEADS, head_dim).astype(jnp.float32)
    heads_split = qkv_sets.reshape(set_count, members, 3, HEADS, head_dim).astype(jnp.float32)
    queries = heads_split[:, :, 0]
    key_heads = heads_split[:, :, 1]
    values = heads_split[:, :, 2]
    weight_grad = jnp.einsum('smhd,snhd->shmn', mixed_grad, values)
    low_weights = rounded(softmax_weights).astype(jnp.float32)
    value_grad = jnp.einsum('shmn,smhd->snhd', low_weights, mixed_grad)
    centre = lax.optimization_barrier(jnp.sum(softmax_weights * weight_grad, axis=-1, keepdims=True))
    score_grad = rounded(softmax_weights * (weight_grad - centre) / math.sqrt(head_dim)).astype(jnp.float32)
    query_grad = jnp.einsum('shmn,snhd->smhd', score_grad, key_heads)
    key_grad = jnp.einsum('shmn,smhd->snhd', score_grad, queries)
    qkv_grad_sets = rounded(jnp.stack([query_grad, key_grad, value_grad], axis=2).reshape(set_count, members, 3 * channels))
    qkv_part = outer_sum(normed_sets, qkv_grad_sets)
    normed_grad = rounded(dense_transposed(qkv_grad_sets, qkv_weight))
    return (qkv_part, mix_part, normed_grad)

def to_grid(image):
    height, grid_width, channels = image.shape
    shaped = image.reshape(GRID, height // GRID, GRID, grid_width // GRID, channels)
    return shaped.transpose(1, 3, 0, 2, 4).reshape(-1, GRID * GRID, channels)

def from_grid(sets, height, grid_width):
    channels = sets.shape[-1]
    shaped = sets.reshape(height // GRID, grid_width // GRID, GRID, GRID, channels)
    return shaped.transpose(2, 0, 3, 1, 4).reshape(height, grid_width, channels)

def reference(block_input, cotangent, conv_gain, grid_gain, mlp_gain, expand_weight, depth_kernel, shrink_weight, qkv_weight, mix_weight, grid_bias, widen_weight, narrow_weight):
    height, grid_width, channels = block_input.shape
    band_rows = math.gcd(height, 32)
    band_count = height // band_rows
    starts = jnp.arange(band_count, dtype=jnp.int32) * band_rows
    row_padded = jnp.pad(block_input, ((1, 1), (0, 0), (0, 0)))

    def expand_rows(band_in):
        normed = layer_norm(band_in, conv_gain)
        expand_pre = dense_product(normed, expand_weight)
        return (expand_pre, rounded(gelu_tanh(expand_pre)))

    def conv_rows(first_row):
        band_in = lax.dynamic_slice_in_dim(row_padded, first_row, band_rows + 2, 0)
        expand_pre, expand_act = expand_rows(band_in)
        padded = jnp.pad(expand_act, ((0, 0), (1, 1), (0, 0)))
        depth_pre = depthwise(padded, depth_kernel)
        return (band_in[1:-1], depth_pre, rounded(gelu_tanh(depth_pre)))

    def forward_band(first_row):
        band_in, depth_pre, depth_act = conv_rows(first_row)
        return rounded(band_in.astype(jnp.float32) + dense_product(depth_act, shrink_weight))
    section_one = lax.map(forward_band, starts).reshape(height, grid_width, channels)
    normed_grid = layer_norm(section_one, grid_gain)
    grid_sets = to_grid(normed_grid)
    set_count = grid_sets.shape[0]
    set_block = math.gcd(set_count, 64)
    blocks = set_count // set_block
    set_blocks = grid_sets.reshape(blocks, set_block, GRID * GRID, channels)

    def forward_sets(normed_part):
        return attend(normed_part, qkv_weight, mix_weight, grid_bias)[3]
    projected = lax.map(forward_sets, set_blocks).reshape(set_count, GRID * GRID, channels)
    grid_out = from_grid(projected, height, grid_width)
    section_two = rounded(section_one.astype(jnp.float32) + grid_out.astype(jnp.float32))

    def mlp_band(first_row):
        band_in = lax.dynamic_slice_in_dim(section_two, first_row, band_rows, 0)
        cot_band = lax.dynamic_slice_in_dim(cotangent, first_row, band_rows, 0)
        normed = layer_norm(band_in, mlp_gain)
        widen_pre = dense_product(normed, widen_weight)
        widen_act = rounded(gelu_tanh(widen_pre))
        band_out = rounded(band_in.astype(jnp.float32) + dense_product(widen_act, narrow_weight))
        widen_grad = rounded(dense_transposed(cot_band, narrow_weight) * gelu_slope(widen_pre))
        band_grad = rounded(cot_band.astype(jnp.float32) + norm_back(dense_transposed(widen_grad, widen_weight), band_in, mlp_gain))
        return (band_out, band_grad)
    block_out, section_two_grad = lax.map(mlp_band, starts)
    block_out = block_out.reshape(height, grid_width, channels)
    section_two_grad = section_two_grad.reshape(height, grid_width, channels)
    grad_blocks = to_grid(section_two_grad).reshape(blocks, set_block, GRID * GRID, channels)

    def backward_sets(operands):
        normed_part, grad_part = operands
        qkv_sets, softmax_weights, mixed, unused = attend(normed_part, qkv_weight, mix_weight, grid_bias)
        return attend_back(normed_part, qkv_sets, softmax_weights, mixed, grad_part, qkv_weight, mix_weight)
    qkv_parts, mix_parts, normed_grad_sets = lax.map(backward_sets, (set_blocks, grad_blocks))
    normed_grad = from_grid(normed_grad_sets.reshape(set_count, GRID * GRID, channels), height, grid_width)
    section_one_grad = rounded(section_two_grad.astype(jnp.float32) + norm_back(normed_grad, section_one, grid_gain))

    def shrink_back(first_row):
        band_in, depth_pre, depth_act = conv_rows(first_row)
        cot_band = lax.dynamic_slice_in_dim(section_one_grad, first_row, band_rows, 0)
        return rounded(dense_transposed(cot_band, shrink_weight) * gelu_slope(depth_pre))
    depth_grad = lax.map(shrink_back, starts).reshape(height, grid_width, -1)
    grad_padded = jnp.pad(depth_grad, ((1, 1), (1, 1), (0, 0)))

    def expand_back(first_row):
        grad_band = lax.dynamic_slice_in_dim(grad_padded, first_row, band_rows + 2, 0)
        hidden_grad = depth_back(grad_band, depth_kernel)
        band_in = lax.dynamic_slice_in_dim(block_input, first_row, band_rows, 0)
        expand_pre, expand_act = expand_rows(band_in)
        expand_grad = rounded(hidden_grad * gelu_slope(expand_pre))
        cot_band = lax.dynamic_slice_in_dim(section_one_grad, first_row, band_rows, 0)
        return rounded(cot_band.astype(jnp.float32) + norm_back(dense_transposed(expand_grad, expand_weight), band_in, conv_gain))
    input_grad = lax.map(expand_back, starts).reshape(height, grid_width, channels)
    factor = 1.0 / math.sqrt(height * grid_width)
    qkv_grad = lax.optimization_barrier(jnp.sum(qkv_parts, axis=0)) * factor
    mix_grad = lax.optimization_barrier(jnp.sum(mix_parts, axis=0)) * factor
    return (block_out, input_grad, qkv_grad, mix_grad)
```

```python
import functools
import math

import jax
import jax.numpy as jnp
from jax import lax
from jax.experimental import pallas as pl
from jax.experimental.pallas import tpu as pltpu
from jax.sharding import PartitionSpec as P

F32 = jnp.float32
BF16 = jnp.bfloat16
MESH = pl.DeviceIdType.MESH
HEADS = 8
EPS = 1e-05
C0 = 0.7978845608028654
C1 = 0.7978845608028654 * 0.044715
MIB = 1024 * 1024


def mm(left, right):
    return jnp.dot(left, right, preferred_element_type=F32)


def mm_nt(left, right):
    return lax.dot_general(left, right, (((1,), (1,)), ((), ())), preferred_element_type=F32)


def mm_tn(left, right):
    return lax.dot_general(left, right, (((0,), (0,)), ((), ())), preferred_element_type=F32)


def stats(values):
    wide = values.astype(F32)
    centre = wide - jnp.mean(wide, axis=-1, keepdims=True)
    inv = lax.rsqrt(jnp.mean(centre * centre, axis=-1, keepdims=True) + EPS)
    return centre * inv, inv


def norm(values, gain):
    normal, _ = stats(values)
    return (normal * gain).astype(BF16)


def norm_back(cotan, values, gain):
    normal, inv = stats(values)
    scaled = cotan * gain
    return inv * (
        scaled
        - jnp.mean(scaled, axis=-1, keepdims=True)
        - normal * jnp.mean(scaled * normal, axis=-1, keepdims=True)
    )


def gelu_both(u):
    w = C1 * (u * u)
    t = jnp.tanh(u * (w + C0))
    p = 0.5 * t + 0.5
    h = u * p
    slope = p + (h * (1.0 - p)) * (6.0 * w + 2.0 * C0)
    return h, slope


def kernel(
    x_ref, cot_ref, cg_ref, gg_ref, mg_ref, we_ref, kf_ref, ws_ref, wqkv_ref, wmix_ref, bias_ref,
    ww_ref, wn_ref, perm_ref,
    out_ref, grad_ref, qg_ref, mxg_ref,
    h_ref, s1_ref, s2_ref, blk_ref, side_ref, halo_ref, hh_ref, xcol_ref, colf_ref, edge_ref,
    x1_ref, n2h_ref, rb_ref, n2s_ref, qs_ref, ks_ref, vs_ref, ps_ref, mxs_ref, mx_ref, mh_ref,
    x2_ref, h3_ref, dx2_ref, dm_ref, rb2_ref, dns_ref, dq_ref, dk_ref, dv_ref, dn_ref, dnh_ref, dx1_ref,
    drow_ref, dcol_ref, dcorn_ref, ccol_ref, g_ref, gb_ref, r1_ref, t1_ref, r2_ref, a3_ref, a4_ref,
    ssem, rsem, hs_sem, hr_sem, ds_sem, dr_sem, as_sem, ar_sem,
):
    row = lax.axis_index("row")
    col = lax.axis_index("col")
    core = lax.rem(row, 2)
    gi = lax.div(row, 2)
    me = gi * 8 + col
    px = lax.div(gi, 4) * 2 + lax.rem(col, 2)
    py = lax.rem(gi, 4)
    pz = lax.div(col, 2)
    nrow, ncol = 16, 8

    halo_ref[...] = jnp.zeros(halo_ref.shape, BF16)
    xcol_ref[...] = jnp.zeros(xcol_ref.shape, BF16)
    drow_ref[...] = jnp.zeros(drow_ref.shape, BF16)
    dcol_ref[...] = jnp.zeros(dcol_ref.shape, BF16)
    dcorn_ref[...] = jnp.zeros(dcorn_ref.shape, BF16)

    barrier = pltpu.get_barrier_semaphore()

    def greet(t, carry):
        r = lax.rem(row + lax.div(t, ncol), nrow)
        c = lax.rem(col + lax.rem(t, ncol), ncol)
        pl.semaphore_signal(barrier, inc=1, device_id=(r, c), device_id_type=MESH)
        return carry

    lax.fori_loop(1, nrow * ncol, greet, 0)

    for i in range(32):
        colf_ref[0, i : i + 1, 0:256] = x_ref[4 * i].astype(F32)[0:1]
        colf_ref[1, i : i + 1, 0:256] = x_ref[4 * i + 3].astype(F32)[15:16]
    xcol_ref[0] = colf_ref[0, :, 0:256].astype(BF16)
    xcol_ref[1] = colf_ref[1, :, 0:256].astype(BF16)

    cg = cg_ref[...]
    gg = gg_ref[...]
    mg = mg_ref[...]

    def expand_block(b, carry):
        n1 = norm(x_ref[pl.ds(16 * b, 16)].reshape(256, 256), cg)
        for l in range(4):
            lanes = slice(256 * l, 256 * l + 256)
            h, slope = gelu_both(mm(n1, we_ref[:, lanes]))
            h_ref[pl.ds(1 + 4 * b, 4), :, lanes] = h.astype(BF16).reshape(4, 64, 256)
            s1_ref[pl.ds(4 * b, 4), :, lanes] = slope.astype(BF16).reshape(4, 64, 256)
        return carry

    lax.fori_loop(0, 4, expand_block, 0)
    pl.semaphore_wait(barrier, nrow * ncol - 1)

    def neighbours(edge, send, source, target, s_sem, r_sem):
        for idx, dr, dc in edge:
            there_r, there_c = row + dr, col + dc
            ok = (there_r >= 0) & (there_r < nrow) & (there_c >= 0) & (there_c < ncol)
            back_r, back_c = row - dr, col - dc
            ok_back = (back_r >= 0) & (back_r < nrow) & (back_c >= 0) & (back_c < ncol)
            copy = pltpu.make_async_remote_copy(
                src_ref=source(idx), dst_ref=target(idx), send_sem=s_sem.at[idx],
                recv_sem=r_sem.at[idx], device_id=(there_r, there_c), device_id_type=MESH,
            )
            if send == 0:
                pl.when(ok)(copy.start)
            elif send == 1:
                pl.when(ok_back)(copy.wait_recv)
            else:
                pl.when(ok)(copy.wait_send)

    edges = (
        (0, -1, 0), (1, 1, 0), (2, 0, -1), (3, 0, 1),
        (4, -1, -1), (5, -1, 1), (6, 1, -1), (7, 1, 1),
    )

    def x_source(idx):
        return (
            x_ref.at[pl.ds(0, 4)], x_ref.at[pl.ds(124, 4)], xcol_ref.at[0], xcol_ref.at[1],
            x_ref.at[0], x_ref.at[3], x_ref.at[124], x_ref.at[127],
        )[idx]

    def x_target(idx):
        return (
            halo_ref.at[pl.ds(4, 4)], halo_ref.at[pl.ds(0, 4)], xcol_ref.at[3], xcol_ref.at[2],
            halo_ref.at[15], halo_ref.at[14], halo_ref.at[13], halo_ref.at[12],
        )[idx]

    neighbours(edges, 0, x_source, x_target, hs_sem, hr_sem)
    lax.fori_loop(4, 8, expand_block, 0)
    neighbours(edges, 1, x_source, x_target, hs_sem, hr_sem)

    halo_ref[8:10] = xcol_ref[2].reshape(2, 16, 256)
    halo_ref[10:12] = xcol_ref[3].reshape(2, 16, 256)
    n1 = norm(halo_ref[...].reshape(256, 256), cg)
    for l in range(4):
        lanes = slice(256 * l, 256 * l + 256)
        h, _ = gelu_both(mm(n1, we_ref[:, lanes]))
        hh_ref[:, lanes] = h.astype(BF16)
    h_ref[0] = hh_ref[0:64]
    h_ref[33] = hh_ref[64:128]

    rows32 = lax.broadcasted_iota(jnp.int32, (32, 1024), 0)

    def side(place, mid, above, below, taps):
        up = jnp.where(rows32 == 0, above, pltpu.roll(mid, 1, 0))
        down = jnp.where(rows32 == 31, below, pltpu.roll(mid, 31, 0))
        whole = (
            kf_ref[taps[0] : taps[0] + 1] * up
            + kf_ref[taps[1] : taps[1] + 1] * mid
            + kf_ref[taps[2] : taps[2] + 1] * down
        )
        for i in range(32):
            side_ref[place, i] = whole[i : i + 1]

    side(
        0,
        hh_ref[128:160].astype(F32),
        hh_ref[192:208].astype(F32)[15:16],
        hh_ref[224:240].astype(F32)[15:16],
        (0, 3, 6),
    )
    side(
        1,
        hh_ref[160:192].astype(F32),
        hh_ref[208:224].astype(F32)[0:1],
        hh_ref[240:256].astype(F32)[0:1],
        (2, 5, 8),
    )

    io64 = lax.broadcasted_iota(jnp.int32, (64, 128), 0)

    def depthwise(r, lanes, taps):
        a0 = h_ref[r, :, lanes].astype(F32)
        a1 = h_ref[r + 1, :, lanes].astype(F32)
        a2 = h_ref[r + 2, :, lanes].astype(F32)

        def three(j):
            return (
                kf_ref[taps[j] : taps[j] + 1, lanes] * a0
                + kf_ref[taps[3 + j] : taps[3 + j] + 1, lanes] * a1
                + kf_ref[taps[6 + j] : taps[6 + j] + 1, lanes] * a2
            )

        left = jnp.where(io64 == 0, side_ref[0, r, :, lanes], pltpu.roll(three(0), 1, 0))
        right = jnp.where(io64 == 63, side_ref[1, r, :, lanes], pltpu.roll(three(2), 63, 0))
        return three(1) + left + right

    forward_taps = tuple(range(9))
    backward_taps = tuple(range(8, -1, -1))

    def a2a_start(src, dst, k, q):
        pltpu.make_async_copy(src.at[64 * k + me], dst.at[64 * k + me], rsem.at[q, k]).start()

        def step(t, carry):
            qx = lax.rem(px + lax.rem(t, 4), 4)
            qy = lax.rem(py + lax.rem(lax.div(t, 4), 4), 4)
            qz = lax.rem(pz + lax.div(t, 16), 4)
            pg = lax.div(qx, 2) * 4 + qy
            pe = qz * 2 + lax.rem(qx, 2)
            pltpu.make_async_remote_copy(
                src_ref=src.at[64 * k + pg * 8 + pe],
                dst_ref=dst.at[64 * k + me],
                send_sem=ssem.at[q, k],
                recv_sem=rsem.at[q, k],
                device_id=(2 * pg + core, pe),
                device_id_type=MESH,
            ).start()
            return carry

        lax.fori_loop(1, 64, step, 0)

    def a2a_wait(dst, k, q):
        whole = dst.at[pl.ds(64 * k, 64)]
        pltpu.make_async_copy(whole, whole, rsem.at[q, k]).wait()

    def a2a_wait_send(src, k, q):
        part = src.at[pl.ds(64 * k, 63)]
        pltpu.make_async_copy(part, part, ssem.at[q, k]).wait()

    def shrink_block(b, carry):
        def one_row(rr, inner):
            r = 4 * b + rr
            for l in range(8):
                lanes = slice(128 * l, 128 * l + 128)
                h2, slope = gelu_both(depthwise(r, lanes, forward_taps))
                blk_ref[rr, :, lanes] = h2.astype(BF16)
                s2_ref[r, :, lanes] = slope.astype(BF16)
            return inner

        lax.fori_loop(0, 4, one_row, 0)
        here = pl.ds(16 * b, 16)
        added = mm(blk_ref[...].reshape(256, 1024), ws_ref[...])
        x1 = (x_ref[here].reshape(256, 256).astype(F32) + added).astype(BF16)
        x1_ref[here] = x1.reshape(16, 16, 256)
        n2h_ref[here] = norm(x1, gg).reshape(16, 16, 256)
        return carry

    for k in range(2):
        lax.fori_loop(4 * k, 4 * k + 4, shrink_block, 0)
        a2a_start(n2h_ref, rb_ref, k, 0)

    perm = perm_ref
    lane_head = lax.broadcasted_iota(jnp.int32, (64, 256), 1) // 32
    masks = [(lane_head == h).astype(F32) for h in range(HEADS)]
    masks_low = [m.astype(BF16) for m in masks]

    def spread(values):
        return jnp.concatenate([values * masks_low[h] for h in range(HEADS)], axis=0)

    def fold(product):
        total = product[0:64] * masks[0]
        for h in range(1, HEADS):
            total = total + product[64 * h : 64 * h + 64] * masks[h]
        return total

    def to_sets(src, dst, k):
        for i in range(4):
            block = src[64 * k + 16 * i : 64 * k + 16 * i + 16].reshape(256, 256)
            dst[16 * k : 16 * k + 16, 16 * i : 16 * i + 16, :] = (
                mm(perm[...], block).astype(BF16).reshape(16, 16, 256)
            )

    def from_sets(src, dst, k):
        for i in range(4):
            block = src[16 * k : 16 * k + 16, 16 * i : 16 * i + 16, :].reshape(256, 256)
            dst[64 * k + 16 * i : 64 * k + 16 * i + 16] = (
                mm(perm[...], block).astype(BF16).reshape(16, 16, 256)
            )

    scale = 1.0 / math.sqrt(32.0)

    def attend_set(s, carry):
        q_blk = spread(qs_ref[s])
        scores = mm_nt(ks_ref[s], q_blk) * scale + bias_ref[...]
        top = jnp.max(scores, axis=0, keepdims=True)
        e = jnp.exp(scores - top)
        probs = e * (1.0 / jnp.sum(e, axis=0, keepdims=True))
        ps_ref[s] = probs
        mxs_ref[s] = fold(mm_tn(probs.astype(BF16), vs_ref[s])).astype(BF16)
        return carry

    for k in range(2):
        a2a_wait(rb_ref, k, 0)
        to_sets(rb_ref, n2s_ref, k)

        def qkv_block(i, carry):
            here = pl.ds(16 * k + 4 * i, 4)
            n2 = n2s_ref[here].reshape(256, 256)
            qs_ref[here] = mm(n2, wqkv_ref[:, 0:256]).astype(BF16).reshape(4, 64, 256)
            ks_ref[here] = mm(n2, wqkv_ref[:, 256:512]).astype(BF16).reshape(4, 64, 256)
            vs_ref[here] = mm(n2, wqkv_ref[:, 512:768]).astype(BF16).reshape(4, 64, 256)
            return carry

        lax.fori_loop(0, 4, qkv_block, 0)
        lax.fori_loop(16 * k, 16 * k + 16, attend_set, 0)
        from_sets(mxs_ref, mx_ref, k)
        a2a_start(mx_ref, mh_ref, k, 1)

    def mlp_block(b, carry):
        here = pl.ds(16 * b, 16)
        attended = mm(mh_ref[here].reshape(256, 256), wmix_ref[...]).astype(BF16)
        x2 = (x1_ref[here].reshape(256, 256).astype(F32) + attended.astype(F32)).astype(BF16)
        x2_ref[here] = x2.reshape(16, 16, 256)
        n3 = norm(x2, mg)
        cot = cot_ref[here].reshape(256, 256)
        back = jnp.zeros((256, 256), F32)
        for l in range(4):
            lanes = slice(256 * l, 256 * l + 256)
            h3, slope = gelu_both(mm(n3, ww_ref[:, lanes]))
            h3_ref[pl.ds(4 * b, 4), :, lanes] = h3.astype(BF16).reshape(4, 64, 256)
            du3 = (mm_nt(cot, wn_ref[lanes, :]) * slope).astype(BF16)
            back = back + mm_nt(du3, ww_ref[:, lanes])
        dx2 = (cot.astype(F32) + norm_back(back, x2, mg)).astype(BF16)
        dx2_ref[here] = dx2.reshape(16, 16, 256)
        dm_ref[here] = mm_nt(dx2, wmix_ref[...]).astype(BF16).reshape(16, 16, 256)
        return carry

    for k in range(2):
        a2a_wait(mh_ref, k, 1)
        lax.fori_loop(4 * k, 4 * k + 4, mlp_block, 0)
        a2a_start(dm_ref, rb2_ref, k, 2)

    def out_block(b, carry):
        here = pl.ds(16 * b, 16)
        h3 = h3_ref[pl.ds(4 * b, 4)].reshape(256, 1024)
        out = x2_ref[here].reshape(256, 256).astype(F32) + mm(h3, wn_ref[...])
        out_ref[here] = out.astype(BF16).reshape(16, 16, 256)
        return carry

    lax.fori_loop(0, 8, out_block, 0)
    g_ref[:, 768:1024] = mm_tn(
        mh_ref[...].reshape(2048, 256), dx2_ref[...].reshape(2048, 256)
    )

    def attend_back_set(s, carry):
        q_blk = spread(qs_ref[s])
        d_blk = spread(dns_ref[s])
        probs = ps_ref[s]
        dprobs = mm_nt(vs_ref[s], d_blk)
        centre = jnp.sum(probs * dprobs, axis=0, keepdims=True)
        dscores = (probs * (dprobs - centre) * scale).astype(BF16)
        dv_ref[s] = mm(probs.astype(BF16), d_blk).astype(BF16)
        dk_ref[s] = mm(dscores, q_blk).astype(BF16)
        dq_ref[s] = fold(mm_tn(dscores, ks_ref[s])).astype(BF16)
        return carry

    for k in range(2):
        a2a_wait(rb2_ref, k, 2)
        to_sets(rb2_ref, dns_ref, k)
        lax.fori_loop(16 * k, 16 * k + 16, attend_back_set, 0)

        def dn_block(i, carry):
            here = pl.ds(16 * k + 4 * i, 4)
            total = (
                mm_nt(dq_ref[here].reshape(256, 256), wqkv_ref[:, 0:256])
                + mm_nt(dk_ref[here].reshape(256, 256), wqkv_ref[:, 256:512])
                + mm_nt(dv_ref[here].reshape(256, 256), wqkv_ref[:, 512:768])
            )
            mxs_ref[here] = total.astype(BF16).reshape(4, 64, 256)
            return carry

        lax.fori_loop(0, 4, dn_block, 0)
        from_sets(mxs_ref, dn_ref, k)
        a2a_start(dn_ref, dnh_ref, k, 3)

    n2t = n2s_ref[...].reshape(2048, 256)
    g_ref[:, 0:256] = mm_tn(n2t, dq_ref[...].reshape(2048, 256))
    g_ref[:, 256:512] = mm_tn(n2t, dk_ref[...].reshape(2048, 256))
    g_ref[:, 512:768] = mm_tn(n2t, dv_ref[...].reshape(2048, 256))
    for cb in range(8):
        gb_ref[cb] = g_ref[:, 128 * cb : 128 * cb + 128].astype(BF16).reshape(16, 16, 128)

    def along(axis, count, source, target, q):
        mine = col if axis == 1 else row

        def step(t, carry):
            peer = lax.rem(mine + t, count)
            dev = (row, peer) if axis == 1 else (peer, col)
            pltpu.make_async_remote_copy(
                src_ref=source(peer), dst_ref=target(mine), send_sem=as_sem.at[q],
                recv_sem=ar_sem.at[q], device_id=dev, device_id_type=MESH,
            ).start()
            return carry

        lax.fori_loop(1, count, step, 0)

    def wait_part(ref, sem):
        pltpu.make_async_copy(ref, ref, sem).wait()

    along(1, ncol, lambda p: gb_ref.at[p], lambda m: r1_ref.at[m], 0)
    r1_ref[col] = gb_ref[col]

    def cell_block(b, carry):
        here = pl.ds(16 * b, 16)
        dn = dnh_ref[here].reshape(256, 256).astype(F32)
        x1 = x1_ref[here].reshape(256, 256)
        dx1 = dx2_ref[here].reshape(256, 256).astype(F32) + norm_back(dn, x1, gg)
        dx1 = dx1.astype(BF16)
        dx1_ref[here] = dx1.reshape(16, 16, 256)
        for l in range(4):
            lanes = slice(256 * l, 256 * l + 256)
            slope = s2_ref[pl.ds(4 * b, 4), :, lanes].reshape(256, 256).astype(F32)
            du2 = mm_nt(dx1, ws_ref[lanes, :]) * slope
            h_ref[pl.ds(1 + 4 * b, 4), :, lanes] = du2.astype(BF16).reshape(4, 64, 256)
            for rr in range(4):
                edge_ref[0, 4 * b + rr, :, lanes] = du2[64 * rr : 64 * rr + 1]
                edge_ref[1, 4 * b + rr, :, lanes] = du2[64 * rr + 63 : 64 * rr + 64]
        return carry

    a2a_wait(dnh_ref, 0, 3)
    lax.fori_loop(0, 4, cell_block, 0)
    wait_part(r1_ref.at[pl.ds(0, 7)], ar_sem.at[0])
    total = r1_ref[0].astype(F32)
    for c in range(1, 8):
        total = total + r1_ref[c].astype(F32)
    t1_ref[...] = total.astype(BF16)
    along(0, nrow, lambda p: t1_ref.at[p], lambda m: r2_ref.at[m], 1)
    r2_ref[row] = t1_ref[row]
    a2a_wait(dnh_ref, 1, 3)
    lax.fori_loop(4, 8, cell_block, 0)
    for i in range(32):
        colf_ref[0, i : i + 1] = edge_ref[0, i]
        colf_ref[1, i : i + 1] = edge_ref[1, i]
    ccol_ref[0] = colf_ref[0].astype(BF16)
    ccol_ref[1] = colf_ref[1].astype(BF16)

    def d_source(idx):
        return (
            h_ref.at[1], h_ref.at[32], ccol_ref.at[0], ccol_ref.at[1],
            h_ref.at[1, pl.ds(0, 16)], h_ref.at[1, pl.ds(48, 16)],
            h_ref.at[32, pl.ds(0, 16)], h_ref.at[32, pl.ds(48, 16)],
        )[idx]

    def d_target(idx):
        return (
            drow_ref.at[1], drow_ref.at[0], dcol_ref.at[1], dcol_ref.at[0],
            dcorn_ref.at[3], dcorn_ref.at[2], dcorn_ref.at[1], dcorn_ref.at[0],
        )[idx]

    neighbours(edges, 0, d_source, d_target, ds_sem, dr_sem)

    wait_part(r2_ref.at[pl.ds(0, 15)], ar_sem.at[1])
    total = r2_ref[0].astype(F32)
    for r in range(1, 16):
        total = total + r2_ref[r].astype(F32)
    a3_ref[row] = (total * (1.0 / 512.0)).astype(BF16)
    along(0, nrow, lambda p: a3_ref.at[row], lambda m: a3_ref.at[m], 2)

    neighbours(edges, 1, d_source, d_target, ds_sem, dr_sem)
    h_ref[0] = drow_ref[0]
    h_ref[33] = drow_ref[1]
    side(
        0,
        dcol_ref[0].astype(F32),
        dcorn_ref[0].astype(F32)[15:16],
        dcorn_ref[2].astype(F32)[15:16],
        (8, 5, 2),
    )
    side(
        1,
        dcol_ref[1].astype(F32),
        dcorn_ref[1].astype(F32)[0:1],
        dcorn_ref[3].astype(F32)[0:1],
        (6, 3, 0),
    )

    def input_block(b, carry):
        def one_row(rr, inner):
            r = 4 * b + rr
            for l in range(8):
                lanes = slice(128 * l, 128 * l + 128)
                dh = depthwise(r, lanes, backward_taps)
                blk_ref[rr, :, lanes] = (dh * s1_ref[r, :, lanes].astype(F32)).astype(BF16)
            return inner

        lax.fori_loop(0, 4, one_row, 0)
        here = pl.ds(16 * b, 16)
        back = mm_nt(blk_ref[...].reshape(256, 1024), we_ref[...])
        x = x_ref[here].reshape(256, 256)
        out = dx1_ref[here].reshape(256, 256).astype(F32) + norm_back(back, x, cg)
        grad_ref[here] = out.astype(BF16).reshape(16, 16, 256)
        return carry

    lax.fori_loop(0, 3, input_block, 0)
    wait_part(a3_ref.at[pl.ds(0, 15)], ar_sem.at[2])
    a4_ref[col] = a3_ref[...]
    along(1, ncol, lambda p: a3_ref, lambda m: a4_ref.at[m], 3)
    lax.fori_loop(3, 8, input_block, 0)
    wait_part(a4_ref.at[pl.ds(0, 7)], ar_sem.at[3])
    for cb in range(6):
        qg_ref[:, 128 * cb : 128 * cb + 128] = a4_ref[cb].reshape(256, 128).astype(F32)
    for cb in range(2):
        mxg_ref[:, 128 * cb : 128 * cb + 128] = a4_ref[6 + cb].reshape(256, 128).astype(F32)

    neighbours(edges, 2, x_source, x_target, hs_sem, hr_sem)
    neighbours(edges, 2, d_source, d_target, ds_sem, dr_sem)
    for k in range(2):
        a2a_wait_send(n2h_ref, k, 0)
        a2a_wait_send(mx_ref, k, 1)
        a2a_wait_send(dm_ref, k, 2)
        a2a_wait_send(dn_ref, k, 3)
    wait_part(gb_ref.at[pl.ds(0, 7)], as_sem.at[0])
    wait_part(t1_ref.at[pl.ds(0, 15)], as_sem.at[1])
    wait_part(a3_ref.at[pl.ds(0, 15)], as_sem.at[2])
    wait_part(a4_ref.at[pl.ds(0, 7)], as_sem.at[3])


def body(
    block_input, cotangent, conv_gain, grid_gain, mlp_gain, expand_weight, depth_kernel,
    shrink_weight, qkv_weight, mix_weight, grid_bias, widen_weight, narrow_weight,
):
    taps = jnp.pad(depth_kernel.reshape(9, 1024).astype(F32), ((0, 7), (0, 0)))
    bias = grid_bias.transpose(2, 0, 1).reshape(64, 512)
    place = jnp.arange(256, dtype=jnp.int32)
    perm = (place[None, :] == ((place % 16) * 16 + place // 16)[:, None]).astype(BF16)
    cells = (128, 16, 256)
    sets = (32, 64, 256)
    vm = pltpu.VMEM
    dma = pltpu.SemaphoreType.DMA
    scratch = [
        vm((34, 64, 1024), BF16),
        vm((32, 64, 1024), BF16),
        vm((32, 64, 1024), BF16),
        vm((4, 64, 1024), BF16),
        vm((2, 32, 1, 1024), F32),
        vm((16, 16, 256), BF16),
        vm((256, 1024), BF16),
        vm((4, 32, 256), BF16),
        vm((2, 32, 1024), F32),
        vm((2, 32, 1, 1024), F32),
        vm(cells, BF16),
        vm(cells, BF16),
        vm(cells, BF16),
        vm(sets, BF16),
        vm(sets, BF16),
        vm(sets, BF16),
        vm(sets, BF16),
        vm((32, 64, 512), F32),
        vm(sets, BF16),
        vm(cells, BF16),
        vm(cells, BF16),
        vm(cells, BF16),
        vm((32, 64, 1024), BF16),
        vm(cells, BF16),
        vm(cells, BF16),
        vm(cells, BF16),
        vm(sets, BF16),
        vm(sets, BF16),
        vm(sets, BF16),
        vm(sets, BF16),
        vm(cells, BF16),
        vm(cells, BF16),
        vm(cells, BF16),
        vm((2, 64, 1024), BF16),
        vm((2, 32, 1024), BF16),
        vm((4, 16, 1024), BF16),
        vm((2, 32, 1024), BF16),
        vm((256, 1024), F32),
        vm((8, 16, 16, 128), BF16),
        vm((8, 16, 16, 128), BF16),
        vm((16, 16, 128), BF16),
        vm((16, 16, 128), BF16),
        vm((16, 16, 128), BF16),
        vm((8, 16, 16, 128), BF16),
        dma((4, 2)),
        dma((4, 2)),
        dma((8,)),
        dma((8,)),
        dma((8,)),
        dma((8,)),
        dma((4,)),
        dma((4,)),
    ]
    spec = pl.BlockSpec(memory_space=pltpu.VMEM)
    out, grad, qg, mxg = pl.pallas_call(
        kernel,
        out_shape=(
            jax.ShapeDtypeStruct(cells, BF16),
            jax.ShapeDtypeStruct(cells, BF16),
            jax.ShapeDtypeStruct((256, 768), F32),
            jax.ShapeDtypeStruct((256, 256), F32),
        ),
        in_specs=[spec] * 14,
        out_specs=(spec,) * 4,
        scratch_shapes=scratch,
        compiler_params=pltpu.CompilerParams(
            collective_id=0, has_side_effects=True, vmem_limit_bytes=60 * MIB
        ),
    )(
        block_input.reshape(cells), cotangent.reshape(cells), conv_gain[None], grid_gain[None],
        mlp_gain[None], expand_weight, taps, shrink_weight, qkv_weight, mix_weight, bias,
        widen_weight, narrow_weight, perm,
    )
    return out.reshape(32, 64, 256), grad.reshape(32, 64, 256), qg, mxg


def solution(mesh):
    whole = P()
    tile = P("row", "col", None)
    return jax.shard_map(
        body,
        mesh=mesh,
        in_specs=(tile, tile) + (whole,) * 11,
        out_specs=(tile, tile, whole, whole),
        check_vma=False,
    )
```

```python
import functools
import math

import jax
import jax.numpy as jnp
from jax import lax
from jax.experimental import pallas as pl
from jax.experimental.pallas import tpu as pltpu
from jax.sharding import PartitionSpec as P

F32 = jnp.float32
BF16 = jnp.bfloat16
MESH = pl.DeviceIdType.MESH
HEADS = 8
EPS = 1e-05
C0 = 0.7978845608028654
C1 = 0.7978845608028654 * 0.044715
MIB = 1024 * 1024
GROUP = 4


def mm(left, right):
    return jnp.dot(left, right, preferred_element_type=F32)


def mm_nt(left, right):
    return lax.dot_general(left, right, (((1,), (1,)), ((), ())), preferred_element_type=F32)


def mm_tn(left, right):
    return lax.dot_general(left, right, (((0,), (0,)), ((), ())), preferred_element_type=F32)


def stats(values):
    wide = values.astype(F32)
    centre = wide - jnp.mean(wide, axis=-1, keepdims=True)
    inv = lax.rsqrt(jnp.mean(centre * centre, axis=-1, keepdims=True) + EPS)
    return centre * inv, inv


def norm(values, gain):
    normal, _ = stats(values)
    return (normal * gain).astype(BF16)


def norm_back(cotan, values, gain):
    normal, inv = stats(values)
    scaled = cotan * gain
    return inv * (
        scaled
        - jnp.mean(scaled, axis=-1, keepdims=True)
        - normal * jnp.mean(scaled * normal, axis=-1, keepdims=True)
    )


def gelu_both(wide):
    u = wide.astype(BF16)
    w = C1 * (u * u)
    t = jnp.tanh(u * (w + C0))
    p = 0.5 * t + 0.5
    h = u * p
    slope = p + (h * (1.0 - p)) * (6.0 * w + 2.0 * C0)
    return h, slope


def kernel(
    x_ref, cot_ref, cg_ref, gg_ref, mg_ref, we_ref, kf_ref, ws_ref, wqkv_ref, wmix_ref, bias_ref,
    tap_ref, ww_ref, wn_ref, perm_ref,
    out_ref, grad_ref, qg_ref, mxg_ref,
    h_ref, s1_ref, s2_ref, blk_ref, side_ref, halo_ref, hh_ref, xcol_ref, colf_ref, edge_ref,
    x1_ref, n2h_ref, rb_ref, n2s_ref, qs_ref, ks_ref, vs_ref, ps_ref, mxs_ref, mx_ref, mh_ref,
    x2_ref, h3_ref, dx2_ref, dm_ref, rb2_ref, dns_ref, dq_ref, dk_ref, dv_ref, dn_ref, dnh_ref, dx1_ref,
    drow_ref, dcol_ref, dcorn_ref, ccol_ref, g_ref, gb_ref, r1_ref, t1_ref, r2_ref, a3_ref, a4_ref,
    ssem, rsem, hs_sem, hr_sem, ds_sem, dr_sem, as_sem, ar_sem,
):
    row = lax.axis_index("row")
    col = lax.axis_index("col")
    core = lax.rem(row, 2)
    gi = lax.div(row, 2)
    me = gi * 8 + col
    px = lax.div(gi, 4) * 2 + lax.rem(col, 2)
    py = lax.rem(gi, 4)
    pz = lax.div(col, 2)
    nrow, ncol = 16, 8

    halo_ref[...] = jnp.zeros(halo_ref.shape, BF16)
    xcol_ref[...] = jnp.zeros(xcol_ref.shape, BF16)
    drow_ref[...] = jnp.zeros(drow_ref.shape, BF16)
    dcol_ref[...] = jnp.zeros(dcol_ref.shape, BF16)
    dcorn_ref[...] = jnp.zeros(dcorn_ref.shape, BF16)

    barrier = pltpu.get_barrier_semaphore()

    def greet(t, carry):
        r = lax.rem(row + lax.div(t, ncol), nrow)
        c = lax.rem(col + lax.rem(t, ncol), ncol)
        pl.semaphore_signal(barrier, inc=1, device_id=(r, c), device_id_type=MESH)
        return carry

    lax.fori_loop(1, nrow * ncol, greet, 0)

    for i in range(32):
        colf_ref[0, i : i + 1, 0:256] = x_ref[4 * i].astype(F32)[0:1]
        colf_ref[1, i : i + 1, 0:256] = x_ref[4 * i + 3].astype(F32)[15:16]
    xcol_ref[0] = colf_ref[0, :, 0:256].astype(BF16)
    xcol_ref[1] = colf_ref[1, :, 0:256].astype(BF16)

    cg = cg_ref[...]
    gg = gg_ref[...]
    mg = mg_ref[...]

    def expand_block(b, carry):
        n1 = norm(x_ref[pl.ds(16 * b, 16)].reshape(256, 256), cg)
        for l in range(4):
            lanes = slice(256 * l, 256 * l + 256)
            h, slope = gelu_both(mm(n1, we_ref[:, lanes]))
            h_ref[pl.ds(1 + 4 * b, 4), :, lanes] = h.reshape(4, 64, 256)
            s1_ref[pl.ds(4 * b, 4), :, lanes] = slope.reshape(4, 64, 256)
        return carry

    lax.fori_loop(0, 4, expand_block, 0)
    pl.semaphore_wait(barrier, nrow * ncol - 1)

    def neighbours(edge, send, source, target, s_sem, r_sem):
        for idx, dr, dc in edge:
            there_r, there_c = row + dr, col + dc
            ok = (there_r >= 0) & (there_r < nrow) & (there_c >= 0) & (there_c < ncol)
            back_r, back_c = row - dr, col - dc
            ok_back = (back_r >= 0) & (back_r < nrow) & (back_c >= 0) & (back_c < ncol)
            copy = pltpu.make_async_remote_copy(
                src_ref=source(idx), dst_ref=target(idx), send_sem=s_sem.at[idx],
                recv_sem=r_sem.at[idx], device_id=(there_r, there_c), device_id_type=MESH,
            )
            if send == 0:
                pl.when(ok)(copy.start)
            elif send == 1:
                pl.when(ok_back)(copy.wait_recv)
            else:
                pl.when(ok)(copy.wait_send)

    edges = (
        (0, -1, 0), (1, 1, 0), (2, 0, -1), (3, 0, 1),
        (4, -1, -1), (5, -1, 1), (6, 1, -1), (7, 1, 1),
    )

    def x_source(idx):
        return (
            x_ref.at[pl.ds(0, 4)], x_ref.at[pl.ds(124, 4)], xcol_ref.at[0], xcol_ref.at[1],
            x_ref.at[0], x_ref.at[3], x_ref.at[124], x_ref.at[127],
        )[idx]

    def x_target(idx):
        return (
            halo_ref.at[pl.ds(4, 4)], halo_ref.at[pl.ds(0, 4)], xcol_ref.at[3], xcol_ref.at[2],
            halo_ref.at[15], halo_ref.at[14], halo_ref.at[13], halo_ref.at[12],
        )[idx]

    neighbours(edges, 0, x_source, x_target, hs_sem, hr_sem)
    lax.fori_loop(4, 8, expand_block, 0)
    neighbours(edges, 1, x_source, x_target, hs_sem, hr_sem)

    halo_ref[8:10] = xcol_ref[2].reshape(2, 16, 256)
    halo_ref[10:12] = xcol_ref[3].reshape(2, 16, 256)
    n1 = norm(halo_ref[...].reshape(256, 256), cg)
    for l in range(4):
        lanes = slice(256 * l, 256 * l + 256)
        h, _ = gelu_both(mm(n1, we_ref[:, lanes]))
        hh_ref[:, lanes] = h
    h_ref[0] = hh_ref[0:64]
    h_ref[33] = hh_ref[64:128]

    rows32 = lax.broadcasted_iota(jnp.int32, (32, 1024), 0)

    def side(place, mid, above, below, taps):
        up = jnp.where(rows32 == 0, above, pltpu.roll(mid, 1, 0))
        down = jnp.where(rows32 == 31, below, pltpu.roll(mid, 31, 0))
        whole = (
            kf_ref[taps[0] : taps[0] + 1] * up
            + kf_ref[taps[1] : taps[1] + 1] * mid
            + kf_ref[taps[2] : taps[2] + 1] * down
        )
        for i in range(32):
            side_ref[place, i] = whole[i : i + 1]

    side(
        0,
        hh_ref[128:160].astype(F32),
        hh_ref[192:208].astype(F32)[15:16],
        hh_ref[224:240].astype(F32)[15:16],
        (0, 3, 6),
    )
    side(
        1,
        hh_ref[160:192].astype(F32),
        hh_ref[208:224].astype(F32)[0:1],
        hh_ref[240:256].astype(F32)[0:1],
        (2, 5, 8),
    )

    io8 = lax.broadcasted_iota(jnp.int32, (8, 128), 0)

    def depthwise(r, lanes, taps):
        a0 = h_ref[r, :, lanes].reshape(4, 16, 128)
        a1 = h_ref[r + 1, :, lanes].reshape(4, 16, 128)
        a2 = h_ref[r + 2, :, lanes].reshape(4, 16, 128)

        def three(j):
            total = (
                tap_ref[taps[j], :, lanes][None] * a0
                + tap_ref[taps[3 + j], :, lanes][None] * a1
                + tap_ref[taps[6 + j], :, lanes][None] * a2
            )
            return total.reshape(64, 128).astype(F32)

        left = pltpu.roll(three(0), 1, 0)
        right = pltpu.roll(three(2), 63, 0)
        first = jnp.where(io8 == 0, side_ref[0, r, :, lanes], left[0:8])
        last = jnp.where(io8 == 7, side_ref[1, r, :, lanes], right[56:64])
        left = jnp.concatenate([first, left[8:64]], axis=0)
        right = jnp.concatenate([right[0:56], last], axis=0)
        return three(1) + left + right

    forward_taps = tuple(range(9))
    backward_taps = tuple(range(8, -1, -1))

    def a2a_start(src, dst, k, q):
        pltpu.make_async_copy(src.at[64 * k + me], dst.at[64 * k + me], rsem.at[q, k]).start()

        def step(t, carry):
            qx = lax.rem(px + lax.rem(t, 4), 4)
            qy = lax.rem(py + lax.rem(lax.div(t, 4), 4), 4)
            qz = lax.rem(pz + lax.div(t, 16), 4)
            pg = lax.div(qx, 2) * 4 + qy
            pe = qz * 2 + lax.rem(qx, 2)
            pltpu.make_async_remote_copy(
                src_ref=src.at[64 * k + pg * 8 + pe],
                dst_ref=dst.at[64 * k + me],
                send_sem=ssem.at[q, k],
                recv_sem=rsem.at[q, k],
                device_id=(2 * pg + core, pe),
                device_id_type=MESH,
            ).start()
            return carry

        lax.fori_loop(1, 64, step, 0)

    def a2a_wait(dst, k, q):
        whole = dst.at[pl.ds(64 * k, 64)]
        pltpu.make_async_copy(whole, whole, rsem.at[q, k]).wait()

    def a2a_wait_send(src, k, q):
        part = src.at[pl.ds(64 * k, 63)]
        pltpu.make_async_copy(part, part, ssem.at[q, k]).wait()

    def shrink_block(b, carry):
        def one_row(rr, inner):
            r = 4 * b + rr
            for l in range(8):
                lanes = slice(128 * l, 128 * l + 128)
                h2, slope = gelu_both(depthwise(r, lanes, forward_taps))
                blk_ref[rr, :, lanes] = h2
                s2_ref[r, :, lanes] = slope
            return inner

        lax.fori_loop(0, 4, one_row, 0)
        here = pl.ds(16 * b, 16)
        added = mm(blk_ref[...].reshape(256, 1024), ws_ref[...])
        x1 = (x_ref[here].reshape(256, 256).astype(F32) + added).astype(BF16)
        x1_ref[here] = x1.reshape(16, 16, 256)
        n2h_ref[here] = norm(x1, gg).reshape(16, 16, 256)
        return carry

    for k in range(2):
        lax.fori_loop(4 * k, 4 * k + 4, shrink_block, 0)
        a2a_start(n2h_ref, rb_ref, k, 0)

    perm = perm_ref
    lane_head = lax.broadcasted_iota(jnp.int32, (64, 128), 1) // 32
    masks = [(lane_head == h).astype(F32) for h in range(4)]
    masks_low = [m.astype(BF16) for m in masks]
    halves = ((slice(0, 128), slice(0, 256)), (slice(128, 256), slice(256, 512)))

    def spread(values):
        return jnp.concatenate([values * masks_low[h] for h in range(4)], axis=0)

    def fold(product):
        total = product[0:64] * masks[0]
        for h in range(1, 4):
            total = total + product[64 * h : 64 * h + 64] * masks[h]
        return total

    def to_sets(src, dst, k):
        for i in range(4):
            block = src[64 * k + 16 * i : 64 * k + 16 * i + 16].reshape(256, 256)
            dst[16 * k : 16 * k + 16, 16 * i : 16 * i + 16, :] = (
                mm(perm[...], block).astype(BF16).reshape(16, 16, 256)
            )

    def from_sets(src, dst, k):
        for i in range(4):
            block = src[16 * k : 16 * k + 16, 16 * i : 16 * i + 16, :].reshape(256, 256)
            dst[64 * k + 16 * i : 64 * k + 16 * i + 16] = (
                mm(perm[...], block).astype(BF16).reshape(16, 16, 256)
            )

    scale = 1.0 / math.sqrt(32.0)

    def attend_set(i, carry):
        parts = [(GROUP * i + n, c, w) for n in range(GROUP) for c, w in halves]
        scores = [mm_nt(ks_ref[s, :, c], spread(qs_ref[s, :, c])) for s, c, w in parts]
        low = []
        for (s, c, w), score in zip(parts, scores):
            score = score * scale + bias_ref[:, w]
            e = jnp.exp(score - jnp.max(score, axis=0, keepdims=True))
            probs = e * (1.0 / jnp.sum(e, axis=0, keepdims=True))
            ps_ref[s, :, w] = probs
            low.append(probs.astype(BF16))
        mixed = [mm_tn(p, vs_ref[s, :, c]) for (s, c, w), p in zip(parts, low)]
        for (s, c, w), product in zip(parts, mixed):
            mxs_ref[s, :, c] = fold(product).astype(BF16)
        return carry

    for k in range(2):
        a2a_wait(rb_ref, k, 0)
        to_sets(rb_ref, n2s_ref, k)

        def qkv_block(i, carry):
            here = pl.ds(16 * k + 4 * i, 4)
            n2 = n2s_ref[here].reshape(256, 256)
            qs_ref[here] = mm(n2, wqkv_ref[:, 0:256]).astype(BF16).reshape(4, 64, 256)
            ks_ref[here] = mm(n2, wqkv_ref[:, 256:512]).astype(BF16).reshape(4, 64, 256)
            vs_ref[here] = mm(n2, wqkv_ref[:, 512:768]).astype(BF16).reshape(4, 64, 256)
            return carry

        lax.fori_loop(0, 4, qkv_block, 0)
        lax.fori_loop(16 // GROUP * k, 16 // GROUP * (k + 1), attend_set, 0)
        from_sets(mxs_ref, mx_ref, k)
        a2a_start(mx_ref, mh_ref, k, 1)

    def mlp_block(b, carry):
        here = pl.ds(16 * b, 16)
        attended = mm(mh_ref[here].reshape(256, 256), wmix_ref[...]).astype(BF16)
        x2 = (x1_ref[here].reshape(256, 256).astype(F32) + attended.astype(F32)).astype(BF16)
        x2_ref[here] = x2.reshape(16, 16, 256)
        n3 = norm(x2, mg)
        cot = cot_ref[here].reshape(256, 256)
        back = jnp.zeros((256, 256), F32)
        for l in range(4):
            lanes = slice(256 * l, 256 * l + 256)
            h3, slope = gelu_both(mm(n3, ww_ref[:, lanes]))
            h3_ref[pl.ds(4 * b, 4), :, lanes] = h3.reshape(4, 64, 256)
            du3 = mm_nt(cot, wn_ref[lanes, :]).astype(BF16) * slope
            back = back + mm_nt(du3, ww_ref[:, lanes])
        dx2 = (cot.astype(F32) + norm_back(back, x2, mg)).astype(BF16)
        dx2_ref[here] = dx2.reshape(16, 16, 256)
        dm_ref[here] = mm_nt(dx2, wmix_ref[...]).astype(BF16).reshape(16, 16, 256)
        return carry

    for k in range(2):
        a2a_wait(mh_ref, k, 1)
        lax.fori_loop(4 * k, 4 * k + 4, mlp_block, 0)
        a2a_start(dm_ref, rb2_ref, k, 2)

    def out_block(b, carry):
        here = pl.ds(16 * b, 16)
        h3 = h3_ref[pl.ds(4 * b, 4)].reshape(256, 1024)
        out = x2_ref[here].reshape(256, 256).astype(F32) + mm(h3, wn_ref[...])
        out_ref[here] = out.astype(BF16).reshape(16, 16, 256)
        return carry

    lax.fori_loop(0, 8, out_block, 0)
    g_ref[:, 768:1024] = mm_tn(
        mh_ref[...].reshape(2048, 256), dx2_ref[...].reshape(2048, 256)
    )

    def attend_back_set(i, carry):
        parts = [(GROUP * i + n, c, w) for n in range(GROUP) for c, w in halves]
        d_blk = [spread(dns_ref[s, :, c]) for s, c, w in parts]
        dprobs = [mm_nt(vs_ref[s, :, c], d) for (s, c, w), d in zip(parts, d_blk)]
        dscores = []
        for (s, c, w), dp, d in zip(parts, dprobs, d_blk):
            probs = ps_ref[s, :, w]
            weighted = probs * dp
            centre = jnp.sum(weighted, axis=0, keepdims=True)
            dscores.append(((weighted - probs * centre) * scale).astype(BF16))
            dv_ref[s, :, c] = mm(probs.astype(BF16), d).astype(BF16)
        for (s, c, w), ds in zip(parts, dscores):
            dk_ref[s, :, c] = mm(ds, spread(qs_ref[s, :, c])).astype(BF16)
        folded = [mm_tn(ds, ks_ref[s, :, c]) for (s, c, w), ds in zip(parts, dscores)]
        for (s, c, w), product in zip(parts, folded):
            dq_ref[s, :, c] = fold(product).astype(BF16)
        return carry

    for k in range(2):
        a2a_wait(rb2_ref, k, 2)
        to_sets(rb2_ref, dns_ref, k)
        lax.fori_loop(16 // GROUP * k, 16 // GROUP * (k + 1), attend_back_set, 0)

        def dn_block(i, carry):
            here = pl.ds(16 * k + 4 * i, 4)
            total = (
                mm_nt(dq_ref[here].reshape(256, 256), wqkv_ref[:, 0:256])
                + mm_nt(dk_ref[here].reshape(256, 256), wqkv_ref[:, 256:512])
                + mm_nt(dv_ref[here].reshape(256, 256), wqkv_ref[:, 512:768])
            )
            mxs_ref[here] = total.astype(BF16).reshape(4, 64, 256)
            return carry

        lax.fori_loop(0, 4, dn_block, 0)
        from_sets(mxs_ref, dn_ref, k)
        a2a_start(dn_ref, dnh_ref, k, 3)

    n2t = n2s_ref[...].reshape(2048, 256)
    g_ref[:, 0:256] = mm_tn(n2t, dq_ref[...].reshape(2048, 256))
    g_ref[:, 256:512] = mm_tn(n2t, dk_ref[...].reshape(2048, 256))
    g_ref[:, 512:768] = mm_tn(n2t, dv_ref[...].reshape(2048, 256))
    for cb in range(8):
        gb_ref[cb] = g_ref[:, 128 * cb : 128 * cb + 128].astype(BF16).reshape(16, 16, 128)

    def along(axis, count, source, target, q):
        mine = col if axis == 1 else row

        def step(t, carry):
            peer = lax.rem(mine + t, count)
            dev = (row, peer) if axis == 1 else (peer, col)
            pltpu.make_async_remote_copy(
                src_ref=source(peer), dst_ref=target(mine), send_sem=as_sem.at[q],
                recv_sem=ar_sem.at[q], device_id=dev, device_id_type=MESH,
            ).start()
            return carry

        lax.fori_loop(1, count, step, 0)

    def wait_part(ref, sem):
        pltpu.make_async_copy(ref, ref, sem).wait()

    along(1, ncol, lambda p: gb_ref.at[p], lambda m: r1_ref.at[m], 0)
    r1_ref[col] = gb_ref[col]

    def cell_block(b, carry):
        here = pl.ds(16 * b, 16)
        dn = dnh_ref[here].reshape(256, 256).astype(F32)
        x1 = x1_ref[here].reshape(256, 256)
        dx1 = dx2_ref[here].reshape(256, 256).astype(F32) + norm_back(dn, x1, gg)
        dx1 = dx1.astype(BF16)
        dx1_ref[here] = dx1.reshape(16, 16, 256)
        for l in range(4):
            lanes = slice(256 * l, 256 * l + 256)
            slope = s2_ref[pl.ds(4 * b, 4), :, lanes].reshape(256, 256)
            du2 = mm_nt(dx1, ws_ref[lanes, :]).astype(BF16) * slope
            h_ref[pl.ds(1 + 4 * b, 4), :, lanes] = du2.reshape(4, 64, 256)
            for rr in range(4):
                edge_ref[0, 4 * b + rr, :, lanes] = du2[64 * rr : 64 * rr + 16].astype(F32)[0:1]
                edge_ref[1, 4 * b + rr, :, lanes] = (
                    du2[64 * rr + 48 : 64 * rr + 64].astype(F32)[15:16]
                )
        return carry

    a2a_wait(dnh_ref, 0, 3)
    lax.fori_loop(0, 4, cell_block, 0)
    wait_part(r1_ref.at[pl.ds(0, 7)], ar_sem.at[0])
    total = r1_ref[0].astype(F32)
    for c in range(1, 8):
        total = total + r1_ref[c].astype(F32)
    t1_ref[...] = total.astype(BF16)
    along(0, nrow, lambda p: t1_ref.at[p], lambda m: r2_ref.at[m], 1)
    r2_ref[row] = t1_ref[row]
    a2a_wait(dnh_ref, 1, 3)
    lax.fori_loop(4, 8, cell_block, 0)
    for i in range(32):
        colf_ref[0, i : i + 1] = edge_ref[0, i]
        colf_ref[1, i : i + 1] = edge_ref[1, i]
    ccol_ref[0] = colf_ref[0].astype(BF16)
    ccol_ref[1] = colf_ref[1].astype(BF16)

    def d_source(idx):
        return (
            h_ref.at[1], h_ref.at[32], ccol_ref.at[0], ccol_ref.at[1],
            h_ref.at[1, pl.ds(0, 16)], h_ref.at[1, pl.ds(48, 16)],
            h_ref.at[32, pl.ds(0, 16)], h_ref.at[32, pl.ds(48, 16)],
        )[idx]

    def d_target(idx):
        return (
            drow_ref.at[1], drow_ref.at[0], dcol_ref.at[1], dcol_ref.at[0],
            dcorn_ref.at[3], dcorn_ref.at[2], dcorn_ref.at[1], dcorn_ref.at[0],
        )[idx]

    neighbours(edges, 0, d_source, d_target, ds_sem, dr_sem)

    wait_part(r2_ref.at[pl.ds(0, 15)], ar_sem.at[1])
    total = r2_ref[0].astype(F32)
    for r in range(1, 16):
        total = total + r2_ref[r].astype(F32)
    a3_ref[row] = (total * (1.0 / 512.0)).astype(BF16)
    along(0, nrow, lambda p: a3_ref.at[row], lambda m: a3_ref.at[m], 2)

    neighbours(edges, 1, d_source, d_target, ds_sem, dr_sem)
    h_ref[0] = drow_ref[0]
    h_ref[33] = drow_ref[1]
    side(
        0,
        dcol_ref[0].astype(F32),
        dcorn_ref[0].astype(F32)[15:16],
        dcorn_ref[2].astype(F32)[15:16],
        (8, 5, 2),
    )
    side(
        1,
        dcol_ref[1].astype(F32),
        dcorn_ref[1].astype(F32)[0:1],
        dcorn_ref[3].astype(F32)[0:1],
        (6, 3, 0),
    )

    def input_block(b, carry):
        def one_row(rr, inner):
            r = 4 * b + rr
            for l in range(8):
                lanes = slice(128 * l, 128 * l + 128)
                dh = depthwise(r, lanes, backward_taps)
                blk_ref[rr, :, lanes] = dh.astype(BF16) * s1_ref[r, :, lanes]
            return inner

        lax.fori_loop(0, 4, one_row, 0)
        here = pl.ds(16 * b, 16)
        back = mm_nt(blk_ref[...].reshape(256, 1024), we_ref[...])
        x = x_ref[here].reshape(256, 256)
        out = dx1_ref[here].reshape(256, 256).astype(F32) + norm_back(back, x, cg)
        grad_ref[here] = out.astype(BF16).reshape(16, 16, 256)
        return carry

    lax.fori_loop(0, 3, input_block, 0)
    wait_part(a3_ref.at[pl.ds(0, 15)], ar_sem.at[2])
    a4_ref[col] = a3_ref[...]
    along(1, ncol, lambda p: a3_ref, lambda m: a4_ref.at[m], 3)
    lax.fori_loop(3, 8, input_block, 0)
    wait_part(a4_ref.at[pl.ds(0, 7)], ar_sem.at[3])
    for cb in range(6):
        qg_ref[:, 128 * cb : 128 * cb + 128] = a4_ref[cb].reshape(256, 128).astype(F32)
    for cb in range(2):
        mxg_ref[:, 128 * cb : 128 * cb + 128] = a4_ref[6 + cb].reshape(256, 128).astype(F32)

    neighbours(edges, 2, x_source, x_target, hs_sem, hr_sem)
    neighbours(edges, 2, d_source, d_target, ds_sem, dr_sem)
    for k in range(2):
        a2a_wait_send(n2h_ref, k, 0)
        a2a_wait_send(mx_ref, k, 1)
        a2a_wait_send(dm_ref, k, 2)
        a2a_wait_send(dn_ref, k, 3)
    wait_part(gb_ref.at[pl.ds(0, 7)], as_sem.at[0])
    wait_part(t1_ref.at[pl.ds(0, 15)], as_sem.at[1])
    wait_part(a3_ref.at[pl.ds(0, 15)], as_sem.at[2])
    wait_part(a4_ref.at[pl.ds(0, 7)], as_sem.at[3])


def body(
    block_input, cotangent, conv_gain, grid_gain, mlp_gain, expand_weight, depth_kernel,
    shrink_weight, qkv_weight, mix_weight, grid_bias, widen_weight, narrow_weight,
):
    taps = jnp.pad(depth_kernel.reshape(9, 1024).astype(F32), ((0, 7), (0, 0)))
    wide_taps = jnp.broadcast_to(depth_kernel.reshape(9, 1, 1024), (9, 16, 1024))
    bias = grid_bias.transpose(2, 0, 1).reshape(64, 512)
    place = jnp.arange(256, dtype=jnp.int32)
    perm = (place[None, :] == ((place % 16) * 16 + place // 16)[:, None]).astype(BF16)
    cells = (128, 16, 256)
    sets = (32, 64, 256)
    vm = pltpu.VMEM
    dma = pltpu.SemaphoreType.DMA
    scratch = [
        vm((34, 64, 1024), BF16),
        vm((32, 64, 1024), BF16),
        vm((32, 64, 1024), BF16),
        vm((4, 64, 1024), BF16),
        vm((2, 32, 1, 1024), F32),
        vm((16, 16, 256), BF16),
        vm((256, 1024), BF16),
        vm((4, 32, 256), BF16),
        vm((2, 32, 1024), F32),
        vm((2, 32, 1, 1024), F32),
        vm(cells, BF16),
        vm(cells, BF16),
        vm(cells, BF16),
        vm(sets, BF16),
        vm(sets, BF16),
        vm(sets, BF16),
        vm(sets, BF16),
        vm((32, 64, 512), F32),
        vm(sets, BF16),
        vm(cells, BF16),
        vm(cells, BF16),
        vm(cells, BF16),
        vm((32, 64, 1024), BF16),
        vm(cells, BF16),
        vm(cells, BF16),
        vm(cells, BF16),
        vm(sets, BF16),
        vm(sets, BF16),
        vm(sets, BF16),
        vm(sets, BF16),
        vm(cells, BF16),
        vm(cells, BF16),
        vm(cells, BF16),
        vm((2, 64, 1024), BF16),
        vm((2, 32, 1024), BF16),
        vm((4, 16, 1024), BF16),
        vm((2, 32, 1024), BF16),
        vm((256, 1024), F32),
        vm((8, 16, 16, 128), BF16),
        vm((8, 16, 16, 128), BF16),
        vm((16, 16, 128), BF16),
        vm((16, 16, 128), BF16),
        vm((16, 16, 128), BF16),
        vm((8, 16, 16, 128), BF16),
        dma((4, 2)),
        dma((4, 2)),
        dma((8,)),
        dma((8,)),
        dma((8,)),
        dma((8,)),
        dma((4,)),
        dma((4,)),
    ]
    spec = pl.BlockSpec(memory_space=pltpu.VMEM)
    out, grad, qg, mxg = pl.pallas_call(
        kernel,
        out_shape=(
            jax.ShapeDtypeStruct(cells, BF16),
            jax.ShapeDtypeStruct(cells, BF16),
            jax.ShapeDtypeStruct((256, 768), F32),
            jax.ShapeDtypeStruct((256, 256), F32),
        ),
        in_specs=[spec] * 15,
        out_specs=(spec,) * 4,
        scratch_shapes=scratch,
        compiler_params=pltpu.CompilerParams(
            collective_id=0, has_side_effects=True, vmem_limit_bytes=60 * MIB
        ),
    )(
        block_input.reshape(cells), cotangent.reshape(cells), conv_gain[None], grid_gain[None],
        mlp_gain[None], expand_weight, taps, shrink_weight, qkv_weight, mix_weight, bias, wide_taps,
        widen_weight, narrow_weight, perm,
    )
    return out.reshape(32, 64, 256), grad.reshape(32, 64, 256), qg, mxg


def solution(mesh):
    whole = P()
    tile = P("row", "col", None)
    return jax.shard_map(
        body,
        mesh=mesh,
        in_specs=(tile, tile) + (whole,) * 11,
        out_specs=(tile, tile, whole, whole),
        check_vma=False,
    )
```

```python
import functools
import math

import jax
import jax.numpy as jnp
from jax import lax
from jax.experimental import pallas as pl
from jax.experimental.pallas import tpu as pltpu
from jax.sharding import PartitionSpec as P

F32 = jnp.float32
BF16 = jnp.bfloat16
MESH = pl.DeviceIdType.MESH
HEADS = 8
EPS = 1e-05
C0 = 0.7978845608028654
C1 = 0.7978845608028654 * 0.044715
MIB = 1024 * 1024
GROUP = 4


def mm(left, right):
    return jnp.dot(left, right, preferred_element_type=F32)


def mm_nt(left, right):
    return lax.dot_general(left, right, (((1,), (1,)), ((), ())), preferred_element_type=F32)


def mm_tn(left, right):
    return lax.dot_general(left, right, (((0,), (0,)), ((), ())), preferred_element_type=F32)


def stats(values):
    wide = values.astype(F32)
    centre = wide - jnp.mean(wide, axis=-1, keepdims=True)
    inv = lax.rsqrt(jnp.mean(centre * centre, axis=-1, keepdims=True) + EPS)
    return centre * inv, inv


def norm(values, gain):
    normal, _ = stats(values)
    return (normal * gain).astype(BF16)


def norm_back(cotan, values, gain):
    normal, inv = stats(values)
    scaled = cotan * gain
    return inv * (
        scaled
        - jnp.mean(scaled, axis=-1, keepdims=True)
        - normal * jnp.mean(scaled * normal, axis=-1, keepdims=True)
    )


def gelu_both(wide):
    u = wide.astype(BF16)
    w = C1 * (u * u)
    t = jnp.tanh(u * (w + C0))
    p = 0.5 * t + 0.5
    h = u * p
    slope = p + (h * (1.0 - p)) * (6.0 * w + 2.0 * C0)
    return h, slope


def kernel(
    x_ref, cot_ref, cg_ref, gg_ref, mg_ref, we_ref, kd_ref, ws_ref, wqkv_ref, wmix_ref,
    heads_ref, ww_ref, wn_ref,
    out_hbm, grad_hbm, qg_hbm, mxg_hbm,
    out_ref, grad_ref, qg_ref, mxg_ref, out_sem,
    h_ref, s1_ref, s2_ref, blk_ref, side_ref, halo_ref, hh_ref, xcol_ref, colf_ref, edge_ref,
    x1_ref, n2h_ref, rb_ref, n2s_ref, qs_ref, ks_ref, vs_ref, ps_ref, mxs_ref, mx_ref, mh_ref,
    x2_ref, h3_ref, dx2_ref, dm_ref, rb2_ref, dns_ref, dq_ref, dk_ref, dv_ref, dn_ref, dnh_ref, dx1_ref,
    drow_ref, dcol_ref, dcorn_ref, ccol_ref, g_ref, gb_ref, r1_ref, t1_ref, r2_ref, a3_ref, a4_ref,
    kf_ref, perm, bias_ref,
    ssem, rsem, hs_sem, hr_sem, ds_sem, dr_sem, as_sem, ar_sem,
):
    row = lax.axis_index("row")
    col = lax.axis_index("col")
    core = lax.rem(row, 2)
    gi = lax.div(row, 2)
    me = gi * 8 + col
    px = lax.div(gi, 4) * 2 + lax.rem(col, 2)
    py = lax.rem(gi, 4)
    pz = lax.div(col, 2)
    nrow, ncol = 16, 8

    halo_ref[...] = jnp.zeros(halo_ref.shape, BF16)
    xcol_ref[...] = jnp.zeros(xcol_ref.shape, BF16)
    drow_ref[...] = jnp.zeros(drow_ref.shape, BF16)
    dcol_ref[...] = jnp.zeros(dcol_ref.shape, BF16)
    dcorn_ref[...] = jnp.zeros(dcorn_ref.shape, BF16)

    barrier = pltpu.get_barrier_semaphore()

    def greet(r, c):
        pl.semaphore_signal(barrier, inc=1, device_id=(r, c), device_id_type=MESH)

    def greet_core(t, carry):
        greet(lax.rem(row + 2 * lax.div(t, 8), nrow), lax.rem(col + lax.rem(t, 8), ncol))
        return carry

    lax.fori_loop(1, 64, greet_core, 0)
    for t in range(8):
        greet(lax.rem(row + 1 + 2 * t, nrow), col)
    for dr in (-1, 1):
        for dc in (-1, 1):
            there_r, there_c = row + dr, col + dc
            ok = (there_r >= 0) & (there_r < nrow) & (there_c >= 0) & (there_c < ncol)
            pl.when(ok)(functools.partial(greet, there_r, there_c))
    rows_near = jnp.where((row == 0) | (row == nrow - 1), 1, 2)
    cols_near = jnp.where((col == 0) | (col == ncol - 1), 1, 2)
    greeted = 63 + 8 + rows_near * cols_near

    for i in range(32):
        colf_ref[0, i : i + 1, 0:256] = x_ref[4 * i].astype(F32)[0:1]
        colf_ref[1, i : i + 1, 0:256] = x_ref[4 * i + 3].astype(F32)[15:16]
    xcol_ref[0] = colf_ref[0, :, 0:256].astype(BF16)
    xcol_ref[1] = colf_ref[1, :, 0:256].astype(BF16)

    cg = cg_ref[...]
    gg = gg_ref[...]
    mg = mg_ref[...]

    def expand_block(b, carry):
        n1 = norm(x_ref[pl.ds(16 * b, 16)].reshape(256, 256), cg)
        for l in range(4):
            lanes = slice(256 * l, 256 * l + 256)
            h, slope = gelu_both(mm(n1, we_ref[:, lanes]))
            h_ref[pl.ds(1 + 4 * b, 4), :, lanes] = h.reshape(4, 64, 256)
            s1_ref[pl.ds(4 * b, 4), :, lanes] = slope.reshape(4, 64, 256)
        return carry

    lax.fori_loop(0, 4, expand_block, 0)
    pl.semaphore_wait(barrier, greeted)

    def neighbours(edge, send, source, target, s_sem, r_sem):
        for idx, dr, dc in edge:
            there_r, there_c = row + dr, col + dc
            ok = (there_r >= 0) & (there_r < nrow) & (there_c >= 0) & (there_c < ncol)
            back_r, back_c = row - dr, col - dc
            ok_back = (back_r >= 0) & (back_r < nrow) & (back_c >= 0) & (back_c < ncol)
            copy = pltpu.make_async_remote_copy(
                src_ref=source(idx), dst_ref=target(idx), send_sem=s_sem.at[idx],
                recv_sem=r_sem.at[idx], device_id=(there_r, there_c), device_id_type=MESH,
            )
            if send == 0:
                pl.when(ok)(copy.start)
            elif send == 1:
                pl.when(ok_back)(copy.wait_recv)
            else:
                pl.when(ok)(copy.wait_send)

    edges = (
        (0, -1, 0), (1, 1, 0), (2, 0, -1), (3, 0, 1),
        (4, -1, -1), (5, -1, 1), (6, 1, -1), (7, 1, 1),
    )

    def x_source(idx):
        return (
            x_ref.at[pl.ds(0, 4)], x_ref.at[pl.ds(124, 4)], xcol_ref.at[0], xcol_ref.at[1],
            x_ref.at[0], x_ref.at[3], x_ref.at[124], x_ref.at[127],
        )[idx]

    def x_target(idx):
        return (
            halo_ref.at[pl.ds(4, 4)], halo_ref.at[pl.ds(0, 4)], xcol_ref.at[3], xcol_ref.at[2],
            halo_ref.at[15], halo_ref.at[14], halo_ref.at[13], halo_ref.at[12],
        )[idx]

    neighbours(edges, 0, x_source, x_target, hs_sem, hr_sem)

    def narrow_block(b, carry):
        cot = cot_ref[pl.ds(16 * b, 16)].reshape(256, 256)
        for l in range(4):
            lanes = slice(256 * l, 256 * l + 256)
            back = mm_nt(cot, wn_ref[lanes, :]).astype(BF16)
            h3_ref[pl.ds(4 * b, 4), :, lanes] = back.reshape(4, 64, 256)
        return carry

    lax.fori_loop(4, 8, expand_block, 0)
    for i in range(3):
        taps = kd_ref[i].astype(F32)
        for j in range(3):
            tap = taps[j : j + 1]
            kf_ref[3 * i + j : 3 * i + j + 1] = tap
    at = lax.broadcasted_iota(jnp.int32, (256, 256), 0)
    to = lax.broadcasted_iota(jnp.int32, (256, 256), 1)
    perm[...] = jnp.where(to == (at % 16) * 16 + at // 16, 1.0, 0.0).astype(BF16)
    for j in range(4):
        pair = [heads_ref[2 * j + n].T for n in range(2)]
        bias_ref[:, 128 * j : 128 * j + 128] = jnp.concatenate(pair, axis=1)
    lax.fori_loop(0, 8, narrow_block, 0)
    neighbours(edges, 1, x_source, x_target, hs_sem, hr_sem)

    halo_ref[8:10] = xcol_ref[2].reshape(2, 16, 256)
    halo_ref[10:12] = xcol_ref[3].reshape(2, 16, 256)
    n1 = norm(halo_ref[...].reshape(256, 256), cg)
    for l in range(4):
        lanes = slice(256 * l, 256 * l + 256)
        h, _ = gelu_both(mm(n1, we_ref[:, lanes]))
        hh_ref[:, lanes] = h
    h_ref[0] = hh_ref[0:64]
    h_ref[33] = hh_ref[64:128]

    rows32 = lax.broadcasted_iota(jnp.int32, (32, 1024), 0)

    def side(which, mid, above, below, taps, keep=(0, 32)):
        size = mid.shape[0]
        rows = rows32[0:size]
        up = jnp.where(rows == 0, above, pltpu.roll(mid, 1, 0))
        down = jnp.where(rows == size - 1, below, pltpu.roll(mid, size - 1, 0))
        whole = (
            kf_ref[taps[0] : taps[0] + 1] * up
            + kf_ref[taps[1] : taps[1] + 1] * mid
            + kf_ref[taps[2] : taps[2] + 1] * down
        )
        for i in range(*keep):
            side_ref[which, i] = whole[i : i + 1]

    side(
        0,
        hh_ref[128:160].astype(F32),
        hh_ref[192:208].astype(F32)[15:16],
        hh_ref[224:240].astype(F32)[15:16],
        (0, 3, 6),
    )
    side(
        1,
        hh_ref[160:192].astype(F32),
        hh_ref[208:224].astype(F32)[0:1],
        hh_ref[240:256].astype(F32)[0:1],
        (2, 5, 8),
    )

    io8 = lax.broadcasted_iota(jnp.int32, (8, 128), 0)

    def depthwise(r, lanes, taps):
        a0 = h_ref[r, :, lanes].astype(F32)
        a1 = h_ref[r + 1, :, lanes].astype(F32)
        a2 = h_ref[r + 2, :, lanes].astype(F32)

        def three(j):
            return (
                kf_ref[taps[j] : taps[j] + 1, lanes] * a0
                + kf_ref[taps[3 + j] : taps[3 + j] + 1, lanes] * a1
                + kf_ref[taps[6 + j] : taps[6 + j] + 1, lanes] * a2
            )

        left = pltpu.roll(three(0), 1, 0)
        right = pltpu.roll(three(2), 63, 0)
        first = jnp.where(io8 == 0, side_ref[0, r, :, lanes], left[0:8])
        last = jnp.where(io8 == 7, side_ref[1, r, :, lanes], right[56:64])
        left = jnp.concatenate([first, left[8:64]], axis=0)
        right = jnp.concatenate([right[0:56], last], axis=0)
        return three(1) + left + right

    forward_taps = tuple(range(9))
    backward_taps = tuple(range(8, -1, -1))

    place = 16 * lax.rem(col, 4) + 2 * gi + lax.div(col, 4)
    zh = lax.div(col, 4)
    xh = lax.div(gi, 4)

    def send_piece(src, dst, at, k, q, dev):
        pltpu.make_async_remote_copy(
            src_ref=src.at[at], dst_ref=dst.at[64 * k + me], send_sem=ssem.at[q, k],
            recv_sem=rsem.at[q, k], device_id=dev, device_id_type=MESH,
        ).start()

    step2 = [(xh, zh), (1 - xh, 1 - zh)]
    step4 = [(lax.rem(px + t, 4), lax.rem(py + t, 4), lax.rem(pz + t, 4)) for t in range(4)]
    along_x = [(lax.div(s[0], 2), lax.rem(s[0], 2)) for s in step4]

    def send_block(src, dst, b, q):
        k, part = lax.div(b, 4), lax.rem(b, 4)
        for t in range(1, 16):
            og = step2[t % 2][0] * 4 + step4[t // 4][1]
            oz = step2[(t // 2) % 2][1]
            send_piece(src, dst, 16 * b + 2 * og + oz, k, q, (2 * og + core, 4 * oz + part))

    def send_rest(src, dst, k, q):
        for t in range(1, 4):
            part = lax.rem(col + t, 4)
            at = 64 * k + 16 * part + 2 * gi + zh
            send_piece(src, dst, at, k, q, (row, 4 * zh + part))
        pltpu.make_async_copy(src.at[64 * k + place], dst.at[64 * k + me], rsem.at[q, k]).start()

    def send_home(src, dst, k, q):
        pltpu.make_async_copy(src.at[64 * k + me], dst.at[64 * k + place], rsem.at[q, k]).start()

        for t in range(1, 64):
            (hi, lo), qy, qz = along_x[t % 4], step4[t // 4 % 4][1], step4[t // 16][2]
            pg = hi * 4 + qy
            pe = qz * 2 + lo
            pltpu.make_async_remote_copy(
                src_ref=src.at[64 * k + pg * 8 + pe],
                dst_ref=dst.at[64 * k + place],
                send_sem=ssem.at[q, k],
                recv_sem=rsem.at[q, k],
                device_id=(2 * pg + core, pe),
                device_id_type=MESH,
            ).start()

    def a2a_wait(dst, k, q):
        whole = dst.at[pl.ds(64 * k, 64)]
        pltpu.make_async_copy(whole, whole, rsem.at[q, k]).wait()

    def a2a_wait_send(src, k, q):
        part = src.at[pl.ds(64 * k, 63)]
        pltpu.make_async_copy(part, part, ssem.at[q, k]).wait()

    def shrink_block(b, carry, before=True):
        def one_row(rr, inner):
            r = 4 * b + rr
            for l in range(8):
                lanes = slice(128 * l, 128 * l + 128)
                h2, slope = gelu_both(depthwise(r, lanes, forward_taps))
                blk_ref[rr, :, lanes] = h2
                s2_ref[r, :, lanes] = slope
            return inner

        lax.fori_loop(0, 4, one_row, 0)
        here = pl.ds(16 * b, 16)
        if before:
            send_block(n2h_ref, rb_ref, b - 1, 0)
        added = mm(blk_ref[...].reshape(256, 1024), ws_ref[...])
        x1 = (x_ref[here].reshape(256, 256).astype(F32) + added).astype(BF16)
        x1_ref[here] = x1.reshape(16, 16, 256)
        n2h_ref[here] = norm(x1, gg).reshape(16, 16, 256)
        return carry

    shrink_block(0, 0, before=False)
    lax.fori_loop(1, 8, shrink_block, 0)
    send_rest(n2h_ref, rb_ref, 0, 0)
    send_block(n2h_ref, rb_ref, 7, 0)
    send_rest(n2h_ref, rb_ref, 1, 0)

    lane_head = lax.broadcasted_iota(jnp.int32, (64, 128), 1) // 32
    masks = [(lane_head == h).astype(F32) for h in range(4)]
    masks_low = [m.astype(BF16) for m in masks]
    halves = ((slice(0, 128), slice(0, 256)), (slice(128, 256), slice(256, 512)))

    def spread(values):
        return jnp.concatenate([values * masks_low[h] for h in range(4)], axis=0)

    def fold(product):
        total = product[0:64] * masks[0]
        for h in range(1, 4):
            total = total + product[64 * h : 64 * h + 64] * masks[h]
        return total

    def to_sets(src, dst, k):
        for i in range(4):
            block = src[64 * k + 16 * i : 64 * k + 16 * i + 16].reshape(256, 256)
            dst[16 * k : 16 * k + 16, 16 * i : 16 * i + 16, :] = (
                mm(perm[...], block).astype(BF16).reshape(16, 16, 256)
            )

    def from_sets(src, dst, k):
        for i in range(4):
            block = src[16 * k : 16 * k + 16, 16 * i : 16 * i + 16, :].reshape(256, 256)
            dst[64 * k + 16 * i : 64 * k + 16 * i + 16] = (
                mm(perm[...], block).astype(BF16).reshape(16, 16, 256)
            )

    scale = 1.0 / math.sqrt(32.0)

    def attend_set(i, carry):
        parts = [(GROUP * i + n, c, w) for n in range(GROUP) for c, w in halves]
        scores = [mm_nt(ks_ref[s, :, c], spread(qs_ref[s, :, c])) for s, c, w in parts]
        low = []
        for (s, c, w), score in zip(parts, scores):
            score = score * scale + bias_ref[:, w]
            e = jnp.exp(score - jnp.max(score, axis=0, keepdims=True))
            probs = e * (1.0 / jnp.sum(e, axis=0, keepdims=True))
            ps_ref[s, :, w] = probs
            low.append(probs.astype(BF16))
        mixed = [mm_tn(p, vs_ref[s, :, c]) for (s, c, w), p in zip(parts, low)]
        for (s, c, w), product in zip(parts, mixed):
            mxs_ref[s, :, c] = fold(product).astype(BF16)
        return carry

    for k in range(2):
        a2a_wait(rb_ref, k, 0)
        to_sets(rb_ref, n2s_ref, k)

        def qkv_block(i, carry):
            here = pl.ds(16 * k + 4 * i, 4)
            n2 = n2s_ref[here].reshape(256, 256)
            qs_ref[here] = mm(n2, wqkv_ref[:, 0:256]).astype(BF16).reshape(4, 64, 256)
            ks_ref[here] = mm(n2, wqkv_ref[:, 256:512]).astype(BF16).reshape(4, 64, 256)
            vs_ref[here] = mm(n2, wqkv_ref[:, 512:768]).astype(BF16).reshape(4, 64, 256)
            return carry

        lax.fori_loop(0, 4, qkv_block, 0)
        lax.fori_loop(16 // GROUP * k, 16 // GROUP * (k + 1), attend_set, 0)
        from_sets(mxs_ref, mx_ref, k)
        send_home(mx_ref, mh_ref, k, 1)

    def mlp_block(b, carry, before=True):
        here = pl.ds(16 * b, 16)
        if before:
            send_block(dm_ref, rb2_ref, b - 1, 2)
        attended = mm(mh_ref[here].reshape(256, 256), wmix_ref[...]).astype(BF16)
        x2 = (x1_ref[here].reshape(256, 256).astype(F32) + attended.astype(F32)).astype(BF16)
        x2_ref[here] = x2.reshape(16, 16, 256)
        n3 = norm(x2, mg)
        cot = cot_ref[here].reshape(256, 256)
        back = jnp.zeros((256, 256), F32)
        for l in range(4):
            lanes = slice(256 * l, 256 * l + 256)
            h3, slope = gelu_both(mm(n3, ww_ref[:, lanes]))
            rows = pl.ds(4 * b, 4)
            du3 = h3_ref[rows, :, lanes].reshape(256, 256) * slope
            h3_ref[rows, :, lanes] = h3.reshape(4, 64, 256)
            back = back + mm_nt(du3, ww_ref[:, lanes])
        dx2 = (cot.astype(F32) + norm_back(back, x2, mg)).astype(BF16)
        dx2_ref[here] = dx2.reshape(16, 16, 256)
        dm_ref[here] = mm_nt(dx2, wmix_ref[...]).astype(BF16).reshape(16, 16, 256)
        return carry

    for k in range(2):
        a2a_wait(mh_ref, k, 1)
        mlp_block(4 * k, 0, before=False)
        lax.fori_loop(4 * k + 1, 4 * k + 4, mlp_block, 0)
        send_block(dm_ref, rb2_ref, 4 * k + 3, 2)
        send_rest(dm_ref, rb2_ref, k, 2)

    def out_block(b, carry):
        here = pl.ds(16 * b, 16)
        h3 = h3_ref[pl.ds(4 * b, 4)].reshape(256, 1024)
        out = x2_ref[here].reshape(256, 256).astype(F32) + mm(h3, wn_ref[...])
        out_ref[here] = out.astype(BF16).reshape(16, 16, 256)
        return carry

    lax.fori_loop(0, 8, out_block, 0)
    store_out = pltpu.make_async_copy(out_ref, out_hbm, out_sem.at[8])
    store_out.start()
    g_ref[:, 768:1024] = mm_tn(
        mh_ref[...].reshape(2048, 256), dx2_ref[...].reshape(2048, 256)
    )

    def attend_back_set(i, carry):
        parts = [(GROUP * i + n, c, w) for n in range(GROUP) for c, w in halves]
        d_blk = [spread(dns_ref[s, :, c]) for s, c, w in parts]
        dprobs = [mm_nt(vs_ref[s, :, c], d) for (s, c, w), d in zip(parts, d_blk)]
        dscores = []
        for (s, c, w), dp, d in zip(parts, dprobs, d_blk):
            probs = ps_ref[s, :, w]
            weighted = probs * dp
            centre = jnp.sum(weighted, axis=0, keepdims=True)
            dscores.append(((weighted - probs * centre) * scale).astype(BF16))
            dv_ref[s, :, c] = mm(probs.astype(BF16), d).astype(BF16)
        for (s, c, w), ds in zip(parts, dscores):
            dk_ref[s, :, c] = mm(ds, spread(qs_ref[s, :, c])).astype(BF16)
        folded = [mm_tn(ds, ks_ref[s, :, c]) for (s, c, w), ds in zip(parts, dscores)]
        for (s, c, w), product in zip(parts, folded):
            dq_ref[s, :, c] = fold(product).astype(BF16)
        return carry

    for k in range(2):
        a2a_wait(rb2_ref, k, 2)
        to_sets(rb2_ref, dns_ref, k)
        lax.fori_loop(16 // GROUP * k, 16 // GROUP * (k + 1), attend_back_set, 0)

        def dn_block(i, carry):
            here = pl.ds(16 * k + 4 * i, 4)
            total = (
                mm_nt(dq_ref[here].reshape(256, 256), wqkv_ref[:, 0:256])
                + mm_nt(dk_ref[here].reshape(256, 256), wqkv_ref[:, 256:512])
                + mm_nt(dv_ref[here].reshape(256, 256), wqkv_ref[:, 512:768])
            )
            mxs_ref[here] = total.astype(BF16).reshape(4, 64, 256)
            return carry

        lax.fori_loop(0, 4, dn_block, 0)
        from_sets(mxs_ref, dn_ref, k)
        send_home(dn_ref, dnh_ref, k, 3)

    n2t = n2s_ref[...].reshape(2048, 256)
    g_ref[:, 0:256] = mm_tn(n2t, dq_ref[...].reshape(2048, 256))
    g_ref[:, 256:512] = mm_tn(n2t, dk_ref[...].reshape(2048, 256))
    g_ref[:, 512:768] = mm_tn(n2t, dv_ref[...].reshape(2048, 256))
    for cb in range(8):
        gb_ref[cb] = g_ref[:, 128 * cb : 128 * cb + 128].astype(BF16).reshape(16, 16, 128)

    def along(axis, count, source, target, q):
        mine = col if axis == 1 else row

        def step(t, carry):
            peer = lax.rem(mine + t, count)
            dev = (row, peer) if axis == 1 else (peer, col)
            pltpu.make_async_remote_copy(
                src_ref=source(peer), dst_ref=target(mine), send_sem=as_sem.at[q],
                recv_sem=ar_sem.at[q], device_id=dev, device_id_type=MESH,
            ).start()
            return carry

        lax.fori_loop(1, count, step, 0)

    def wait_part(ref, sem):
        pltpu.make_async_copy(ref, ref, sem).wait()

    along(1, ncol, lambda p: gb_ref.at[p], lambda m: r1_ref.at[m], 0)
    r1_ref[col] = gb_ref[col]

    def cell_block(b, carry):
        here = pl.ds(16 * b, 16)
        dn = dnh_ref[here].reshape(256, 256).astype(F32)
        x1 = x1_ref[here].reshape(256, 256)
        dx1 = dx2_ref[here].reshape(256, 256).astype(F32) + norm_back(dn, x1, gg)
        dx1 = dx1.astype(BF16)
        dx1_ref[here] = dx1.reshape(16, 16, 256)
        for l in range(4):
            lanes = slice(256 * l, 256 * l + 256)
            slope = s2_ref[pl.ds(4 * b, 4), :, lanes].reshape(256, 256)
            du2 = mm_nt(dx1, ws_ref[lanes, :]).astype(BF16) * slope
            h_ref[pl.ds(1 + 4 * b, 4), :, lanes] = du2.reshape(4, 64, 256)
            for rr in range(4):
                edge_ref[0, 4 * b + rr, :, lanes] = du2[64 * rr : 64 * rr + 16].astype(F32)[0:1]
                edge_ref[1, 4 * b + rr, :, lanes] = (
                    du2[64 * rr + 48 : 64 * rr + 64].astype(F32)[15:16]
                )
        return carry

    def store_grad(b):
        here = pl.ds(16 * b, 16)
        return pltpu.make_async_copy(grad_ref.at[here], grad_hbm.at[here], out_sem.at[b])

    def input_block(b, carry):
        def one_row(rr, inner):
            r = 4 * b + rr
            for l in range(8):
                lanes = slice(128 * l, 128 * l + 128)
                dh = depthwise(r, lanes, backward_taps)
                blk_ref[rr, :, lanes] = dh.astype(BF16) * s1_ref[r, :, lanes]
            return inner

        lax.fori_loop(0, 4, one_row, 0)
        here = pl.ds(16 * b, 16)
        back = mm_nt(blk_ref[...].reshape(256, 1024), we_ref[...])
        x = x_ref[here].reshape(256, 256)
        out = dx1_ref[here].reshape(256, 256).astype(F32) + norm_back(back, x, cg)
        grad_ref[here] = out.astype(BF16).reshape(16, 16, 256)
        store_grad(b).start()
        return carry

    d_edges = edges + ((8, 0, -1), (9, 0, 1))

    def d_source(idx):
        return (
            h_ref.at[1], h_ref.at[32], ccol_ref.at[0, pl.ds(16, 16)], ccol_ref.at[1, pl.ds(16, 16)],
            h_ref.at[1, pl.ds(0, 16)], h_ref.at[1, pl.ds(48, 16)],
            h_ref.at[32, pl.ds(0, 16)], h_ref.at[32, pl.ds(48, 16)],
            ccol_ref.at[0, pl.ds(0, 16)], ccol_ref.at[1, pl.ds(0, 16)],
        )[idx]

    def d_target(idx):
        return (
            drow_ref.at[1], drow_ref.at[0],
            dcol_ref.at[1, pl.ds(16, 16)], dcol_ref.at[0, pl.ds(16, 16)],
            dcorn_ref.at[3], dcorn_ref.at[2], dcorn_ref.at[1], dcorn_ref.at[0],
            dcol_ref.at[1, pl.ds(0, 16)], dcol_ref.at[0, pl.ds(0, 16)],
        )[idx]

    def columns(first):
        for i in range(first, first + 16):
            for n in range(2):
                colf_ref[n, i : i + 1] = edge_ref[n, i]
        for n in range(2):
            ccol_ref[n, first : first + 16] = colf_ref[n, first : first + 16].astype(BF16)

    a2a_wait(dnh_ref, 0, 3)
    lax.fori_loop(0, 4, cell_block, 0)
    columns(0)
    neighbours(d_edges[8:], 0, d_source, d_target, ds_sem, dr_sem)
    wait_part(r1_ref.at[pl.ds(0, 7)], ar_sem.at[0])
    total = r1_ref[0].astype(F32)
    for c in range(1, 8):
        total = total + r1_ref[c].astype(F32)
    t1_ref[...] = total.astype(BF16)
    along(0, nrow, lambda p: t1_ref.at[p], lambda m: r2_ref.at[m], 1)
    r2_ref[row] = t1_ref[row]
    a2a_wait(dnh_ref, 1, 3)
    lax.fori_loop(4, 8, cell_block, 0)
    columns(16)
    neighbours(d_edges[:8], 0, d_source, d_target, ds_sem, dr_sem)
    neighbours(d_edges[8:], 1, d_source, d_target, ds_sem, dr_sem)
    for n, taps in ((0, (8, 5, 2)), (1, (6, 3, 0))):
        early = dcol_ref[n, 0:16].astype(F32)
        side(n, early, early[0:1], early[0:1], taps, (1, 15))
    wait_part(r2_ref.at[pl.ds(0, 15)], ar_sem.at[1])
    total = r2_ref[0].astype(F32)
    for r in range(1, 16):
        total = total + r2_ref[r].astype(F32)
    a3_ref[row] = (total * (1.0 / 512.0)).astype(BF16)
    along(0, nrow, lambda p: a3_ref.at[row], lambda m: a3_ref.at[m], 2)
    lax.fori_loop(1, 3, input_block, 0)
    wait_part(a3_ref.at[pl.ds(0, 15)], ar_sem.at[2])
    a4_ref[col] = a3_ref[...]
    along(1, ncol, lambda p: a3_ref, lambda m: a4_ref.at[m], 3)

    neighbours(d_edges[:8], 1, d_source, d_target, ds_sem, dr_sem)
    h_ref[0] = drow_ref[0]
    h_ref[33] = drow_ref[1]
    side(
        0,
        dcol_ref[0].astype(F32),
        dcorn_ref[0].astype(F32)[15:16],
        dcorn_ref[2].astype(F32)[15:16],
        (8, 5, 2),
    )
    side(
        1,
        dcol_ref[1].astype(F32),
        dcorn_ref[1].astype(F32)[0:1],
        dcorn_ref[3].astype(F32)[0:1],
        (6, 3, 0),
    )

    lax.fori_loop(0, 1, input_block, 0)
    lax.fori_loop(3, 4, input_block, 0)
    lax.fori_loop(4, 8, input_block, 0)
    wait_part(a4_ref.at[pl.ds(0, 7)], ar_sem.at[3])
    for cb in range(6):
        qg_ref[:, 128 * cb : 128 * cb + 128] = a4_ref[cb].reshape(256, 128).astype(F32)
    for cb in range(2):
        mxg_ref[:, 128 * cb : 128 * cb + 128] = a4_ref[6 + cb].reshape(256, 128).astype(F32)

    stores = [
        pltpu.make_async_copy(qg_ref, qg_hbm, out_sem.at[9]),
        pltpu.make_async_copy(mxg_ref, mxg_hbm, out_sem.at[10]),
    ]
    for store in stores:
        store.start()

    neighbours(edges, 2, x_source, x_target, hs_sem, hr_sem)
    neighbours(d_edges, 2, d_source, d_target, ds_sem, dr_sem)
    for k in range(2):
        a2a_wait_send(n2h_ref, k, 0)
        a2a_wait_send(mx_ref, k, 1)
        a2a_wait_send(dm_ref, k, 2)
        a2a_wait_send(dn_ref, k, 3)
    wait_part(gb_ref.at[pl.ds(0, 7)], as_sem.at[0])
    wait_part(t1_ref.at[pl.ds(0, 15)], as_sem.at[1])
    wait_part(a3_ref.at[pl.ds(0, 15)], as_sem.at[2])
    wait_part(a4_ref.at[pl.ds(0, 7)], as_sem.at[3])
    store_out.wait()
    for b in range(8):
        store_grad(b).wait()
    for store in stores:
        store.wait()


def leave(a_in, b_in, c_in, d_in, a_out, b_out, c_out, d_out, a_mid, b_mid, c_mid, d_mid, sem):
    loads, stores = [], []
    for src, mid, dst, parts in (
        (a_in, a_mid, a_out, 4), (b_in, b_mid, b_out, 4), (c_in, c_mid, c_out, 2), (d_in, d_mid, d_out, 1)
    ):
        size = src.shape[0] // parts
        for n in range(parts):
            here = pl.ds(n * size, size)
            at = len(loads)
            loads.append(pltpu.make_async_copy(src.at[here], mid.at[here], sem.at[0, at]))
            stores.append(pltpu.make_async_copy(mid.at[here], dst.at[here], sem.at[1, at]))
    for copy in loads:
        copy.start()
    for load, store in zip(loads, stores):
        load.wait()
        store.start()
    for store in stores:
        store.wait()


def body(
    block_input, cotangent, conv_gain, grid_gain, mlp_gain, expand_weight, depth_kernel,
    shrink_weight, qkv_weight, mix_weight, grid_bias, widen_weight, narrow_weight,
):
    cells = (128, 16, 256)
    sets = (32, 64, 256)
    vm = pltpu.VMEM
    dma = pltpu.SemaphoreType.DMA
    scratch = [
        vm(cells, BF16),
        vm(cells, BF16),
        vm((256, 768), F32),
        vm((256, 256), F32),
        dma((11,)),
        vm((34, 64, 1024), BF16),
        vm((32, 64, 1024), BF16),
        vm((32, 64, 1024), BF16),
        vm((4, 64, 1024), BF16),
        vm((2, 32, 1, 1024), F32),
        vm((16, 16, 256), BF16),
        vm((256, 1024), BF16),
        vm((4, 32, 256), BF16),
        vm((2, 32, 1024), F32),
        vm((2, 32, 1, 1024), F32),
        vm(cells, BF16),
        vm(cells, BF16),
        vm(cells, BF16),
        vm(sets, BF16),
        vm(sets, BF16),
        vm(sets, BF16),
        vm(sets, BF16),
        vm((32, 64, 512), F32),
        vm(sets, BF16),
        vm(cells, BF16),
        vm(cells, BF16),
        vm(cells, BF16),
        vm((32, 64, 1024), BF16),
        vm(cells, BF16),
        vm(cells, BF16),
        vm(cells, BF16),
        vm(sets, BF16),
        vm(sets, BF16),
        vm(sets, BF16),
        vm(sets, BF16),
        vm(cells, BF16),
        vm(cells, BF16),
        vm(cells, BF16),
        vm((2, 64, 1024), BF16),
        vm((2, 32, 1024), BF16),
        vm((4, 16, 1024), BF16),
        vm((2, 32, 1024), BF16),
        vm((256, 1024), F32),
        vm((8, 16, 16, 128), BF16),
        vm((8, 16, 16, 128), BF16),
        vm((16, 16, 128), BF16),
        vm((16, 16, 128), BF16),
        vm((16, 16, 128), BF16),
        vm((8, 16, 16, 128), BF16),
        vm((16, 1024), F32),
        vm((256, 256), BF16),
        vm((64, 512), F32),
        dma((4, 2)),
        dma((4, 2)),
        dma((8,)),
        dma((8,)),
        dma((10,)),
        dma((10,)),
        dma((4,)),
        dma((4,)),
    ]
    spec = pl.BlockSpec(memory_space=pltpu.VMEM)
    anywhere = pl.BlockSpec(memory_space=pl.ANY)
    shapes = (
        jax.ShapeDtypeStruct(cells, BF16),
        jax.ShapeDtypeStruct(cells, BF16),
        jax.ShapeDtypeStruct((256, 768), F32),
        jax.ShapeDtypeStruct((256, 256), F32),
    )
    out, grad, qg, mxg = pl.pallas_call(
        kernel,
        out_shape=shapes,
        in_specs=[spec] * 13,
        out_specs=(anywhere,) * 4,
        scratch_shapes=scratch,
        compiler_params=pltpu.CompilerParams(
            collective_id=0, has_side_effects=True, vmem_limit_bytes=60 * MIB
        ),
    )(
        block_input.reshape(cells), cotangent.reshape(cells), conv_gain[None], grid_gain[None],
        mlp_gain[None], expand_weight, depth_kernel, shrink_weight, qkv_weight, mix_weight, grid_bias,
        widen_weight, narrow_weight,
    )
    held = (out, grad, qg, mxg)
    out, grad, qg, mxg = pl.pallas_call(
        leave,
        out_shape=shapes,
        in_specs=[anywhere] * 4,
        out_specs=(anywhere,) * 4,
        scratch_shapes=[vm(a.shape, a.dtype) for a in shapes] + [dma((2, 12))],
    )(*held)
    return out.reshape(32, 64, 256), grad.reshape(32, 64, 256), qg, mxg


def solution(mesh):
    whole = P()
    tile = P("row", "col", None)
    return jax.shard_map(
        body,
        mesh=mesh,
        in_specs=(tile, tile) + (whole,) * 11,
        out_specs=(tile, tile, whole, whole),
        check_vma=False,
    )
```

```python
import functools
import math

import jax
import jax.numpy as jnp
from jax import lax
from jax.experimental import pallas as pl
from jax.experimental.pallas import tpu as pltpu
from jax.sharding import PartitionSpec as P

F32 = jnp.float32
BF16 = jnp.bfloat16
MESH = pl.DeviceIdType.MESH
HEADS = 8
EPS = 1e-05
C0 = 0.7978845608028654
C1 = 0.7978845608028654 * 0.044715
MIB = 1024 * 1024
GROUP = 8


def mm(left, right):
    return jnp.dot(left, right, preferred_element_type=F32)


def mm_nt(left, right):
    return lax.dot_general(left, right, (((1,), (1,)), ((), ())), preferred_element_type=F32)


def mm_tn(left, right):
    return lax.dot_general(left, right, (((0,), (0,)), ((), ())), preferred_element_type=F32)


def stats(values):
    wide = values.astype(F32)
    centre = wide - jnp.mean(wide, axis=-1, keepdims=True)
    inv = lax.rsqrt(jnp.mean(centre * centre, axis=-1, keepdims=True) + EPS)
    return centre * inv, inv


def norm(values, gain):
    normal, _ = stats(values)
    return (normal * gain).astype(BF16)


def norm_back(cotan, values, gain):
    normal, inv = stats(values)
    scaled = cotan * gain
    return inv * (
        scaled
        - jnp.mean(scaled, axis=-1, keepdims=True)
        - normal * jnp.mean(scaled * normal, axis=-1, keepdims=True)
    )


def gelu_both(wide):
    u = wide.astype(BF16)
    w = C1 * (u * u)
    t = jnp.tanh(u * (w + C0))
    p = 0.5 * t + 0.5
    h = u * p
    slope = p + (h * (1.0 - p)) * (6.0 * w + 2.0 * C0)
    return h, slope


def kernel(
    x_ref, cot_ref, cg_ref, gg_ref, mg_ref, we_ref, kd_ref, ws_ref, wqkv_ref, wmix_ref,
    heads_ref, ww_ref, wn_ref,
    out_hbm, grad_hbm, qg_hbm, mxg_hbm,
    out_ref, grad_ref, qg_ref, mxg_ref, out_sem,
    h_ref, s1_ref, s2_ref, blk_ref, side_ref, halo_ref, hh_ref, xcol_ref, colf_ref, edge_ref,
    x1_ref, n2h_ref, rb_ref, n2s_ref, qs_ref, ks_ref, vs_ref, ps_ref, mxs_ref, mx_ref, mh_ref,
    x2_ref, h3_ref, dx2_ref, dm_ref, rb2_ref, dns_ref, dq_ref, dk_ref, dv_ref, dn_ref, dnh_ref, dx1_ref,
    drow_ref, dcol_ref, dcorn_ref, ccol_ref, g_ref, gb_ref, r1_ref, t1_ref, r2_ref, a3_ref, a4_ref,
    kf_ref, perm, bias_ref,
    ssem, rsem, hs_sem, hr_sem, ds_sem, dr_sem, as_sem, ar_sem,
):
    row = lax.axis_index("row")
    col = lax.axis_index("col")
    core = lax.rem(row, 2)
    gi = lax.div(row, 2)
    me = gi * 8 + col
    px = lax.div(gi, 4) * 2 + lax.rem(col, 2)
    py = lax.rem(gi, 4)
    pz = lax.div(col, 2)
    nrow, ncol = 16, 8

    halo_ref[...] = jnp.zeros(halo_ref.shape, BF16)
    xcol_ref[...] = jnp.zeros(xcol_ref.shape, BF16)
    drow_ref[...] = jnp.zeros(drow_ref.shape, BF16)
    dcol_ref[...] = jnp.zeros(dcol_ref.shape, BF16)
    dcorn_ref[...] = jnp.zeros(dcorn_ref.shape, BF16)

    barrier = pltpu.get_barrier_semaphore()

    def greet(r, c):
        pl.semaphore_signal(barrier, inc=1, device_id=(r, c), device_id_type=MESH)

    def greet_core(t, carry):
        greet(lax.rem(row + 2 * lax.div(t, 8), nrow), lax.rem(col + lax.rem(t, 8), ncol))
        return carry

    lax.fori_loop(1, 64, greet_core, 0)
    for t in range(8):
        greet(lax.rem(row + 1 + 2 * t, nrow), col)
    for dr in (-1, 1):
        for dc in (-1, 1):
            there_r, there_c = row + dr, col + dc
            ok = (there_r >= 0) & (there_r < nrow) & (there_c >= 0) & (there_c < ncol)
            pl.when(ok)(functools.partial(greet, there_r, there_c))
    rows_near = jnp.where((row == 0) | (row == nrow - 1), 1, 2)
    cols_near = jnp.where((col == 0) | (col == ncol - 1), 1, 2)
    greeted = 63 + 8 + rows_near * cols_near

    for i in range(32):
        colf_ref[0, i : i + 1, 0:256] = x_ref[4 * i].astype(F32)[0:1]
        colf_ref[1, i : i + 1, 0:256] = x_ref[4 * i + 3].astype(F32)[15:16]
    xcol_ref[0] = colf_ref[0, :, 0:256].astype(BF16)
    xcol_ref[1] = colf_ref[1, :, 0:256].astype(BF16)

    cg = cg_ref[...]
    gg = gg_ref[...]
    mg = mg_ref[...]

    def expand_block(b, carry):
        n1 = norm(x_ref[pl.ds(64 * b, 64)].reshape(1024, 256), cg)
        for l in range(4):
            lanes = slice(256 * l, 256 * l + 256)
            h, slope = gelu_both(mm(n1, we_ref[:, lanes]))
            h_ref[pl.ds(1 + 16 * b, 16), :, lanes] = h.reshape(16, 64, 256)
            s1_ref[pl.ds(16 * b, 16), :, lanes] = slope.reshape(16, 64, 256)
        return carry

    lax.fori_loop(0, 1, expand_block, 0)
    pl.semaphore_wait(barrier, greeted)

    def neighbours(edge, send, source, target, s_sem, r_sem):
        for idx, dr, dc in edge:
            there_r, there_c = row + dr, col + dc
            ok = (there_r >= 0) & (there_r < nrow) & (there_c >= 0) & (there_c < ncol)
            back_r, back_c = row - dr, col - dc
            ok_back = (back_r >= 0) & (back_r < nrow) & (back_c >= 0) & (back_c < ncol)
            copy = pltpu.make_async_remote_copy(
                src_ref=source(idx), dst_ref=target(idx), send_sem=s_sem.at[idx],
                recv_sem=r_sem.at[idx], device_id=(there_r, there_c), device_id_type=MESH,
            )
            if send == 0:
                pl.when(ok)(copy.start)
            elif send == 1:
                pl.when(ok_back)(copy.wait_recv)
            else:
                pl.when(ok)(copy.wait_send)

    edges = (
        (0, -1, 0), (1, 1, 0), (2, 0, -1), (3, 0, 1),
        (4, -1, -1), (5, -1, 1), (6, 1, -1), (7, 1, 1),
    )

    def x_source(idx):
        return (
            x_ref.at[pl.ds(0, 4)], x_ref.at[pl.ds(124, 4)], xcol_ref.at[0], xcol_ref.at[1],
            x_ref.at[0], x_ref.at[3], x_ref.at[124], x_ref.at[127],
        )[idx]

    def x_target(idx):
        return (
            halo_ref.at[pl.ds(4, 4)], halo_ref.at[pl.ds(0, 4)], xcol_ref.at[3], xcol_ref.at[2],
            halo_ref.at[15], halo_ref.at[14], halo_ref.at[13], halo_ref.at[12],
        )[idx]

    neighbours(edges, 0, x_source, x_target, hs_sem, hr_sem)

    def narrow_block(b, carry):
        cot = cot_ref[pl.ds(64 * b, 64)].reshape(1024, 256)
        for l in range(4):
            lanes = slice(256 * l, 256 * l + 256)
            back = mm_nt(cot, wn_ref[lanes, :]).astype(BF16)
            h3_ref[pl.ds(16 * b, 16), :, lanes] = back.reshape(16, 64, 256)
        return carry

    lax.fori_loop(1, 2, expand_block, 0)
    for i in range(3):
        taps = kd_ref[i].astype(F32)
        for j in range(3):
            tap = taps[j : j + 1]
            kf_ref[3 * i + j : 3 * i + j + 1] = tap
    at = lax.broadcasted_iota(jnp.int32, (256, 256), 0)
    to = lax.broadcasted_iota(jnp.int32, (256, 256), 1)
    perm[...] = jnp.where(to == (at % 16) * 16 + at // 16, 1.0, 0.0).astype(BF16)
    for j in range(4):
        pair = [heads_ref[2 * j + n].T for n in range(2)]
        bias_ref[:, 128 * j : 128 * j + 128] = jnp.concatenate(pair, axis=1)
    lax.fori_loop(0, 2, narrow_block, 0)
    neighbours(edges, 1, x_source, x_target, hs_sem, hr_sem)

    halo_ref[8:10] = xcol_ref[2].reshape(2, 16, 256)
    halo_ref[10:12] = xcol_ref[3].reshape(2, 16, 256)
    n1 = norm(halo_ref[...].reshape(256, 256), cg)
    for l in range(4):
        lanes = slice(256 * l, 256 * l + 256)
        h, _ = gelu_both(mm(n1, we_ref[:, lanes]))
        hh_ref[:, lanes] = h
    h_ref[0] = hh_ref[0:64]
    h_ref[33] = hh_ref[64:128]

    rows32 = lax.broadcasted_iota(jnp.int32, (32, 1024), 0)

    def side(which, mid, above, below, taps, keep=(0, 32)):
        size = mid.shape[0]
        rows = rows32[0:size]
        up = jnp.where(rows == 0, above, pltpu.roll(mid, 1, 0))
        down = jnp.where(rows == size - 1, below, pltpu.roll(mid, size - 1, 0))
        whole = (
            kf_ref[taps[0] : taps[0] + 1] * up
            + kf_ref[taps[1] : taps[1] + 1] * mid
            + kf_ref[taps[2] : taps[2] + 1] * down
        )
        for i in range(*keep):
            side_ref[which, i] = whole[i : i + 1]

    side(
        0,
        hh_ref[128:160].astype(F32),
        hh_ref[192:208].astype(F32)[15:16],
        hh_ref[224:240].astype(F32)[15:16],
        (0, 3, 6),
    )
    side(
        1,
        hh_ref[160:192].astype(F32),
        hh_ref[208:224].astype(F32)[0:1],
        hh_ref[240:256].astype(F32)[0:1],
        (2, 5, 8),
    )

    io8 = lax.broadcasted_iota(jnp.int32, (8, 128), 0)

    def depthwise(r, lanes, taps):
        a0 = h_ref[r, :, lanes].astype(F32)
        a1 = h_ref[r + 1, :, lanes].astype(F32)
        a2 = h_ref[r + 2, :, lanes].astype(F32)

        def three(j):
            return (
                kf_ref[taps[j] : taps[j] + 1, lanes] * a0
                + kf_ref[taps[3 + j] : taps[3 + j] + 1, lanes] * a1
                + kf_ref[taps[6 + j] : taps[6 + j] + 1, lanes] * a2
            )

        left = pltpu.roll(three(0), 1, 0)
        right = pltpu.roll(three(2), 63, 0)
        first = jnp.where(io8 == 0, side_ref[0, r, :, lanes], left[0:8])
        last = jnp.where(io8 == 7, side_ref[1, r, :, lanes], right[56:64])
        left = jnp.concatenate([first, left[8:64]], axis=0)
        right = jnp.concatenate([right[0:56], last], axis=0)
        return three(1) + left + right

    forward_taps = tuple(range(9))
    backward_taps = tuple(range(8, -1, -1))

    place = 16 * lax.rem(col, 4) + 2 * gi + lax.div(col, 4)
    zh = lax.div(col, 4)
    xh = lax.div(gi, 4)

    def send_piece(src, dst, at, k, q, dev):
        pltpu.make_async_remote_copy(
            src_ref=src.at[at], dst_ref=dst.at[64 * k + me], send_sem=ssem.at[q, k],
            recv_sem=rsem.at[q, k], device_id=dev, device_id_type=MESH,
        ).start()

    step2 = [(xh, zh), (1 - xh, 1 - zh)]
    step4 = [(lax.rem(px + t, 4), lax.rem(py + t, 4), lax.rem(pz + t, 4)) for t in range(4)]
    along_x = [(lax.div(s[0], 2), lax.rem(s[0], 2)) for s in step4]

    def send_block(src, dst, b, q):
        k, part = lax.div(b, 4), lax.rem(b, 4)
        for t in range(1, 16):
            og = step2[t % 2][0] * 4 + step4[t // 4][1]
            oz = step2[(t // 2) % 2][1]
            send_piece(src, dst, 16 * b + 2 * og + oz, k, q, (2 * og + core, 4 * oz + part))

    def send_rest(src, dst, k, q):
        for t in range(1, 4):
            part = lax.rem(col + t, 4)
            at = 64 * k + 16 * part + 2 * gi + zh
            send_piece(src, dst, at, k, q, (row, 4 * zh + part))
        pltpu.make_async_copy(src.at[64 * k + place], dst.at[64 * k + me], rsem.at[q, k]).start()

    def send_home(src, dst, k, q):
        pltpu.make_async_copy(src.at[64 * k + me], dst.at[64 * k + place], rsem.at[q, k]).start()

        for t in range(1, 64):
            (hi, lo), qy, qz = along_x[t % 4], step4[t // 4 % 4][1], step4[t // 16][2]
            pg = hi * 4 + qy
            pe = qz * 2 + lo
            pltpu.make_async_remote_copy(
                src_ref=src.at[64 * k + pg * 8 + pe],
                dst_ref=dst.at[64 * k + place],
                send_sem=ssem.at[q, k],
                recv_sem=rsem.at[q, k],
                device_id=(2 * pg + core, pe),
                device_id_type=MESH,
            ).start()

    def a2a_wait(dst, k, q):
        whole = dst.at[pl.ds(64 * k, 64)]
        pltpu.make_async_copy(whole, whole, rsem.at[q, k]).wait()

    def a2a_wait_send(src, k, q):
        part = src.at[pl.ds(64 * k, 63)]
        pltpu.make_async_copy(part, part, ssem.at[q, k]).wait()

    def shrink_block(b, carry, before=True):
        def one_row(rr, inner):
            r = 8 * b + rr
            for l in range(8):
                lanes = slice(128 * l, 128 * l + 128)
                h2, slope = gelu_both(depthwise(r, lanes, forward_taps))
                blk_ref[rr, :, lanes] = h2
                s2_ref[r, :, lanes] = slope
            return inner

        lax.fori_loop(0, 8, one_row, 0)
        here = pl.ds(32 * b, 32)
        if before:
            send_block(n2h_ref, rb_ref, 2 * b - 2, 0)
            send_block(n2h_ref, rb_ref, 2 * b - 1, 0)
        added = mm(blk_ref[...].reshape(512, 1024), ws_ref[...])
        x1 = (x_ref[here].reshape(512, 256).astype(F32) + added).astype(BF16)
        x1_ref[here] = x1.reshape(32, 16, 256)
        n2h_ref[here] = norm(x1, gg).reshape(32, 16, 256)
        return carry

    for k in range(2):
        shrink_block(2 * k, 0, before=False)
        shrink_block(2 * k + 1, 0)
        send_block(n2h_ref, rb_ref, 4 * k + 2, 0)
        send_block(n2h_ref, rb_ref, 4 * k + 3, 0)
        send_rest(n2h_ref, rb_ref, k, 0)

    lane_head = lax.broadcasted_iota(jnp.int32, (64, 128), 1) // 32
    masks = [(lane_head == h).astype(F32) for h in range(4)]
    masks_low = [m.astype(BF16) for m in masks]
    halves = ((slice(0, 128), slice(0, 256)), (slice(128, 256), slice(256, 512)))

    def spread(values):
        return jnp.concatenate([values * masks_low[h] for h in range(4)], axis=0)

    def fold(product):
        total = product[0:64] * masks[0]
        for h in range(1, 4):
            total = total + product[64 * h : 64 * h + 64] * masks[h]
        return total

    def to_sets(src, dst, k):
        for i in range(4):
            block = src[64 * k + 16 * i : 64 * k + 16 * i + 16].reshape(256, 256)
            dst[16 * k : 16 * k + 16, 16 * i : 16 * i + 16, :] = (
                mm(perm[...], block).astype(BF16).reshape(16, 16, 256)
            )

    def from_sets(src, dst, k):
        for i in range(4):
            block = src[16 * k : 16 * k + 16, 16 * i : 16 * i + 16, :].reshape(256, 256)
            dst[64 * k + 16 * i : 64 * k + 16 * i + 16] = (
                mm(perm[...], block).astype(BF16).reshape(16, 16, 256)
            )

    scale = 1.0 / math.sqrt(32.0)

    def attend_set(i, carry):
        parts = [(GROUP * i + n, c, w) for n in range(GROUP) for c, w in halves]
        scores = [mm_nt(ks_ref[s, :, c], spread(qs_ref[s, :, c])) for s, c, w in parts]
        low = []
        for (s, c, w), score in zip(parts, scores):
            score = score * scale + bias_ref[:, w]
            e = jnp.exp(score - jnp.max(score, axis=0, keepdims=True))
            probs = e * (1.0 / jnp.sum(e, axis=0, keepdims=True))
            ps_ref[s, :, w] = probs
            low.append(probs.astype(BF16))
        mixed = [mm_tn(p, vs_ref[s, :, c]) for (s, c, w), p in zip(parts, low)]
        for (s, c, w), product in zip(parts, mixed):
            mxs_ref[s, :, c] = fold(product).astype(BF16)
        return carry

    for k in range(2):
        a2a_wait(rb_ref, k, 0)
        to_sets(rb_ref, n2s_ref, k)

        def qkv_block(i, carry):
            here = pl.ds(16 * k + 8 * i, 8)
            n2 = n2s_ref[here].reshape(512, 256)
            qs_ref[here] = mm(n2, wqkv_ref[:, 0:256]).astype(BF16).reshape(8, 64, 256)
            ks_ref[here] = mm(n2, wqkv_ref[:, 256:512]).astype(BF16).reshape(8, 64, 256)
            vs_ref[here] = mm(n2, wqkv_ref[:, 512:768]).astype(BF16).reshape(8, 64, 256)
            return carry

        lax.fori_loop(0, 2, qkv_block, 0)
        lax.fori_loop(16 // GROUP * k, 16 // GROUP * (k + 1), attend_set, 0)
        from_sets(mxs_ref, mx_ref, k)
        send_home(mx_ref, mh_ref, k, 1)

    def mlp_block(b, carry, before=True):
        here = pl.ds(32 * b, 32)
        if before:
            send_block(dm_ref, rb2_ref, 2 * b - 2, 2)
            send_block(dm_ref, rb2_ref, 2 * b - 1, 2)
        attended = mm(mh_ref[here].reshape(512, 256), wmix_ref[...]).astype(BF16)
        x2 = (x1_ref[here].reshape(512, 256).astype(F32) + attended.astype(F32)).astype(BF16)
        x2_ref[here] = x2.reshape(32, 16, 256)
        n3 = norm(x2, mg)
        cot = cot_ref[here].reshape(512, 256)
        back = jnp.zeros((512, 256), F32)
        for l in range(4):
            lanes = slice(256 * l, 256 * l + 256)
            h3, slope = gelu_both(mm(n3, ww_ref[:, lanes]))
            rows = pl.ds(8 * b, 8)
            du3 = h3_ref[rows, :, lanes].reshape(512, 256) * slope
            h3_ref[rows, :, lanes] = h3.reshape(8, 64, 256)
            back = back + mm_nt(du3, ww_ref[:, lanes])
        dx2 = (cot.astype(F32) + norm_back(back, x2, mg)).astype(BF16)
        dx2_ref[here] = dx2.reshape(32, 16, 256)
        dm_ref[here] = mm_nt(dx2, wmix_ref[...]).astype(BF16).reshape(32, 16, 256)
        return carry

    for k in range(2):
        a2a_wait(mh_ref, k, 1)
        mlp_block(2 * k, 0, before=False)
        mlp_block(2 * k + 1, 0)
        send_block(dm_ref, rb2_ref, 4 * k + 2, 2)
        send_block(dm_ref, rb2_ref, 4 * k + 3, 2)
        send_rest(dm_ref, rb2_ref, k, 2)

    def out_block(b, carry):
        here = pl.ds(64 * b, 64)
        h3 = h3_ref[pl.ds(16 * b, 16)].reshape(1024, 1024)
        out = x2_ref[here].reshape(1024, 256).astype(F32) + mm(h3, wn_ref[...])
        out_ref[here] = out.astype(BF16).reshape(64, 16, 256)
        return carry

    lax.fori_loop(0, 2, out_block, 0)
    store_out = pltpu.make_async_copy(out_ref, out_hbm, out_sem.at[8])
    store_out.start()
    g_ref[:, 768:1024] = mm_tn(
        mh_ref[...].reshape(2048, 256), dx2_ref[...].reshape(2048, 256)
    )

    def attend_back_set(i, carry):
        parts = [(GROUP * i + n, c, w) for n in range(GROUP) for c, w in halves]
        d_blk = [spread(dns_ref[s, :, c]) for s, c, w in parts]
        dprobs = [mm_nt(vs_ref[s, :, c], d) for (s, c, w), d in zip(parts, d_blk)]
        dscores = []
        for (s, c, w), dp, d in zip(parts, dprobs, d_blk):
            probs = ps_ref[s, :, w]
            weighted = probs * dp
            centre = jnp.sum(weighted, axis=0, keepdims=True)
            dscores.append(((weighted - probs * centre) * scale).astype(BF16))
            dv_ref[s, :, c] = mm(probs.astype(BF16), d).astype(BF16)
        for (s, c, w), ds in zip(parts, dscores):
            dk_ref[s, :, c] = mm(ds, spread(qs_ref[s, :, c])).astype(BF16)
        folded = [mm_tn(ds, ks_ref[s, :, c]) for (s, c, w), ds in zip(parts, dscores)]
        for (s, c, w), product in zip(parts, folded):
            dq_ref[s, :, c] = fold(product).astype(BF16)
        return carry

    for k in range(2):
        a2a_wait(rb2_ref, k, 2)
        to_sets(rb2_ref, dns_ref, k)
        lax.fori_loop(16 // GROUP * k, 16 // GROUP * (k + 1), attend_back_set, 0)

        def dn_block(i, carry):
            here = pl.ds(16 * k + 8 * i, 8)
            total = (
                mm_nt(dq_ref[here].reshape(512, 256), wqkv_ref[:, 0:256])
                + mm_nt(dk_ref[here].reshape(512, 256), wqkv_ref[:, 256:512])
                + mm_nt(dv_ref[here].reshape(512, 256), wqkv_ref[:, 512:768])
            )
            mxs_ref[here] = total.astype(BF16).reshape(8, 64, 256)
            return carry

        lax.fori_loop(0, 2, dn_block, 0)
        from_sets(mxs_ref, dn_ref, k)
        send_home(dn_ref, dnh_ref, k, 3)

    n2t = n2s_ref[...].reshape(2048, 256)
    g_ref[:, 0:256] = mm_tn(n2t, dq_ref[...].reshape(2048, 256))
    g_ref[:, 256:512] = mm_tn(n2t, dk_ref[...].reshape(2048, 256))
    g_ref[:, 512:768] = mm_tn(n2t, dv_ref[...].reshape(2048, 256))
    for cb in range(8):
        gb_ref[cb] = g_ref[:, 128 * cb : 128 * cb + 128].astype(BF16).reshape(16, 16, 128)

    def along(axis, count, source, target, q):
        mine = col if axis == 1 else row

        def step(t, carry):
            peer = lax.rem(mine + t, count)
            dev = (row, peer) if axis == 1 else (peer, col)
            pltpu.make_async_remote_copy(
                src_ref=source(peer), dst_ref=target(mine), send_sem=as_sem.at[q],
                recv_sem=ar_sem.at[q], device_id=dev, device_id_type=MESH,
            ).start()
            return carry

        lax.fori_loop(1, count, step, 0)

    def wait_part(ref, sem):
        pltpu.make_async_copy(ref, ref, sem).wait()

    along(1, ncol, lambda p: gb_ref.at[p], lambda m: r1_ref.at[m], 0)
    r1_ref[col] = gb_ref[col]

    def cell_block(b, carry):
        here = pl.ds(32 * b, 32)
        dn = dnh_ref[here].reshape(512, 256).astype(F32)
        x1 = x1_ref[here].reshape(512, 256)
        dx1 = dx2_ref[here].reshape(512, 256).astype(F32) + norm_back(dn, x1, gg)
        dx1 = dx1.astype(BF16)
        dx1_ref[here] = dx1.reshape(32, 16, 256)
        for l in range(4):
            lanes = slice(256 * l, 256 * l + 256)
            slope = s2_ref[pl.ds(8 * b, 8), :, lanes].reshape(512, 256)
            du2 = mm_nt(dx1, ws_ref[lanes, :]).astype(BF16) * slope
            h_ref[pl.ds(1 + 8 * b, 8), :, lanes] = du2.reshape(8, 64, 256)
            for rr in range(8):
                edge_ref[0, 8 * b + rr, :, lanes] = du2[64 * rr : 64 * rr + 16].astype(F32)[0:1]
                edge_ref[1, 8 * b + rr, :, lanes] = (
                    du2[64 * rr + 48 : 64 * rr + 64].astype(F32)[15:16]
                )
        return carry

    def store_grad(b):
        here = pl.ds(16 * b, 16)
        return pltpu.make_async_copy(grad_ref.at[here], grad_hbm.at[here], out_sem.at[b])

    def input_part(first, count):
        cells, pieces = 256 * count, 16 * count

        def one_row(rr, inner):
            r = 4 * first + rr
            for l in range(8):
                lanes = slice(128 * l, 128 * l + 128)
                dh = depthwise(r, lanes, backward_taps)
                blk_ref[rr, :, lanes] = dh.astype(BF16) * s1_ref[r, :, lanes]
            return inner

        lax.fori_loop(0, 4 * count, one_row, 0)
        here = pl.ds(16 * first, pieces)
        back = mm_nt(blk_ref[0 : 4 * count].reshape(cells, 1024), we_ref[...])
        x = x_ref[here].reshape(cells, 256)
        out = dx1_ref[here].reshape(cells, 256).astype(F32) + norm_back(back, x, cg)
        grad_ref[here] = out.astype(BF16).reshape(pieces, 16, 256)
        for b in range(first, first + count):
            store_grad(b).start()

    d_edges = edges + ((8, 0, -1), (9, 0, 1))

    def d_source(idx):
        return (
            h_ref.at[1], h_ref.at[32], ccol_ref.at[0, pl.ds(16, 16)], ccol_ref.at[1, pl.ds(16, 16)],
            h_ref.at[1, pl.ds(0, 16)], h_ref.at[1, pl.ds(48, 16)],
            h_ref.at[32, pl.ds(0, 16)], h_ref.at[32, pl.ds(48, 16)],
            ccol_ref.at[0, pl.ds(0, 16)], ccol_ref.at[1, pl.ds(0, 16)],
        )[idx]

    def d_target(idx):
        return (
            drow_ref.at[1], drow_ref.at[0],
            dcol_ref.at[1, pl.ds(16, 16)], dcol_ref.at[0, pl.ds(16, 16)],
            dcorn_ref.at[3], dcorn_ref.at[2], dcorn_ref.at[1], dcorn_ref.at[0],
            dcol_ref.at[1, pl.ds(0, 16)], dcol_ref.at[0, pl.ds(0, 16)],
        )[idx]

    def columns(first):
        for i in range(first, first + 16):
            for n in range(2):
                colf_ref[n, i : i + 1] = edge_ref[n, i]
        for n in range(2):
            ccol_ref[n, first : first + 16] = colf_ref[n, first : first + 16].astype(BF16)

    a2a_wait(dnh_ref, 0, 3)
    lax.fori_loop(0, 2, cell_block, 0)
    columns(0)
    neighbours(d_edges[8:], 0, d_source, d_target, ds_sem, dr_sem)
    wait_part(r1_ref.at[pl.ds(0, 7)], ar_sem.at[0])
    total = r1_ref[0].astype(F32)
    for c in range(1, 8):
        total = total + r1_ref[c].astype(F32)
    t1_ref[...] = total.astype(BF16)
    along(0, nrow, lambda p: t1_ref.at[p], lambda m: r2_ref.at[m], 1)
    r2_ref[row] = t1_ref[row]
    a2a_wait(dnh_ref, 1, 3)
    lax.fori_loop(2, 4, cell_block, 0)
    columns(16)
    neighbours(d_edges[:8], 0, d_source, d_target, ds_sem, dr_sem)
    neighbours(d_edges[8:], 1, d_source, d_target, ds_sem, dr_sem)
    for n, taps in ((0, (8, 5, 2)), (1, (6, 3, 0))):
        early = dcol_ref[n, 0:16].astype(F32)
        side(n, early, early[0:1], early[0:1], taps, (1, 15))
    wait_part(r2_ref.at[pl.ds(0, 15)], ar_sem.at[1])
    total = r2_ref[0].astype(F32)
    for r in range(1, 16):
        total = total + r2_ref[r].astype(F32)
    a3_ref[row] = (total * (1.0 / 512.0)).astype(BF16)
    along(0, nrow, lambda p: a3_ref.at[row], lambda m: a3_ref.at[m], 2)
    input_part(1, 2)
    wait_part(a3_ref.at[pl.ds(0, 15)], ar_sem.at[2])
    a4_ref[col] = a3_ref[...]
    along(1, ncol, lambda p: a3_ref, lambda m: a4_ref.at[m], 3)

    neighbours(d_edges[:8], 1, d_source, d_target, ds_sem, dr_sem)
    h_ref[0] = drow_ref[0]
    h_ref[33] = drow_ref[1]
    side(
        0,
        dcol_ref[0].astype(F32),
        dcorn_ref[0].astype(F32)[15:16],
        dcorn_ref[2].astype(F32)[15:16],
        (8, 5, 2),
    )
    side(
        1,
        dcol_ref[1].astype(F32),
        dcorn_ref[1].astype(F32)[0:1],
        dcorn_ref[3].astype(F32)[0:1],
        (6, 3, 0),
    )

    input_part(0, 1)
    input_part(3, 2)
    input_part(5, 2)
    input_part(7, 1)
    wait_part(a4_ref.at[pl.ds(0, 7)], ar_sem.at[3])
    for cb in range(6):
        qg_ref[:, 128 * cb : 128 * cb + 128] = a4_ref[cb].reshape(256, 128).astype(F32)
    for cb in range(2):
        mxg_ref[:, 128 * cb : 128 * cb + 128] = a4_ref[6 + cb].reshape(256, 128).astype(F32)

    stores = [
        pltpu.make_async_copy(qg_ref, qg_hbm, out_sem.at[9]),
        pltpu.make_async_copy(mxg_ref, mxg_hbm, out_sem.at[10]),
    ]
    for store in stores:
        store.start()

    neighbours(edges, 2, x_source, x_target, hs_sem, hr_sem)
    neighbours(d_edges, 2, d_source, d_target, ds_sem, dr_sem)
    for k in range(2):
        a2a_wait_send(n2h_ref, k, 0)
        a2a_wait_send(mx_ref, k, 1)
        a2a_wait_send(dm_ref, k, 2)
        a2a_wait_send(dn_ref, k, 3)
    wait_part(gb_ref.at[pl.ds(0, 7)], as_sem.at[0])
    wait_part(t1_ref.at[pl.ds(0, 15)], as_sem.at[1])
    wait_part(a3_ref.at[pl.ds(0, 15)], as_sem.at[2])
    wait_part(a4_ref.at[pl.ds(0, 7)], as_sem.at[3])
    store_out.wait()
    for b in range(8):
        store_grad(b).wait()
    for store in stores:
        store.wait()


def leave(a_in, b_in, c_in, d_in, a_out, b_out, c_out, d_out, a_mid, b_mid, c_mid, d_mid, sem):
    loads, stores = [], []
    for src, mid, dst, parts in (
        (a_in, a_mid, a_out, 4), (b_in, b_mid, b_out, 4), (c_in, c_mid, c_out, 2), (d_in, d_mid, d_out, 1)
    ):
        size = src.shape[0] // parts
        for n in range(parts):
            here = pl.ds(n * size, size)
            at = len(loads)
            loads.append(pltpu.make_async_copy(src.at[here], mid.at[here], sem.at[0, at]))
            stores.append(pltpu.make_async_copy(mid.at[here], dst.at[here], sem.at[1, at]))
    for copy in loads:
        copy.start()
    for load, store in zip(loads, stores):
        load.wait()
        store.start()
    for store in stores:
        store.wait()


def body(
    block_input, cotangent, conv_gain, grid_gain, mlp_gain, expand_weight, depth_kernel,
    shrink_weight, qkv_weight, mix_weight, grid_bias, widen_weight, narrow_weight,
):
    cells = (128, 16, 256)
    sets = (32, 64, 256)
    vm = pltpu.VMEM
    dma = pltpu.SemaphoreType.DMA
    scratch = [
        vm(cells, BF16),
        vm(cells, BF16),
        vm((256, 768), F32),
        vm((256, 256), F32),
        dma((11,)),
        vm((34, 64, 1024), BF16),
        vm((32, 64, 1024), BF16),
        vm((32, 64, 1024), BF16),
        vm((8, 64, 1024), BF16),
        vm((2, 32, 1, 1024), F32),
        vm((16, 16, 256), BF16),
        vm((256, 1024), BF16),
        vm((4, 32, 256), BF16),
        vm((2, 32, 1024), F32),
        vm((2, 32, 1, 1024), F32),
        vm(cells, BF16),
        vm(cells, BF16),
        vm(cells, BF16),
        vm(sets, BF16),
        vm(sets, BF16),
        vm(sets, BF16),
        vm(sets, BF16),
        vm((32, 64, 512), F32),
        vm(sets, BF16),
        vm(cells, BF16),
        vm(cells, BF16),
        vm(cells, BF16),
        vm((32, 64, 1024), BF16),
        vm(cells, BF16),
        vm(cells, BF16),
        vm(cells, BF16),
        vm(sets, BF16),
        vm(sets, BF16),
        vm(sets, BF16),
        vm(sets, BF16),
        vm(cells, BF16),
        vm(cells, BF16),
        vm(cells, BF16),
        vm((2, 64, 1024), BF16),
        vm((2, 32, 1024), BF16),
        vm((4, 16, 1024), BF16),
        vm((2, 32, 1024), BF16),
        vm((256, 1024), F32),
        vm((8, 16, 16, 128), BF16),
        vm((8, 16, 16, 128), BF16),
        vm((16, 16, 128), BF16),
        vm((16, 16, 128), BF16),
        vm((16, 16, 128), BF16),
        vm((8, 16, 16, 128), BF16),
        vm((16, 1024), F32),
        vm((256, 256), BF16),
        vm((64, 512), F32),
        dma((4, 2)),
        dma((4, 2)),
        dma((8,)),
        dma((8,)),
        dma((10,)),
        dma((10,)),
        dma((4,)),
        dma((4,)),
    ]
    spec = pl.BlockSpec(memory_space=pltpu.VMEM)
    anywhere = pl.BlockSpec(memory_space=pl.ANY)
    shapes = (
        jax.ShapeDtypeStruct(cells, BF16),
        jax.ShapeDtypeStruct(cells, BF16),
        jax.ShapeDtypeStruct((256, 768), F32),
        jax.ShapeDtypeStruct((256, 256), F32),
    )
    out, grad, qg, mxg = pl.pallas_call(
        kernel,
        out_shape=shapes,
        in_specs=[spec] * 13,
        out_specs=(anywhere,) * 4,
        scratch_shapes=scratch,
        compiler_params=pltpu.CompilerParams(
            collective_id=0, has_side_effects=True, vmem_limit_bytes=60 * MIB
        ),
    )(
        block_input.reshape(cells), cotangent.reshape(cells), conv_gain[None], grid_gain[None],
        mlp_gain[None], expand_weight, depth_kernel, shrink_weight, qkv_weight, mix_weight, grid_bias,
        widen_weight, narrow_weight,
    )
    held = (out, grad, qg, mxg)
    out, grad, qg, mxg = pl.pallas_call(
        leave,
        out_shape=shapes,
        in_specs=[anywhere] * 4,
        out_specs=(anywhere,) * 4,
        scratch_shapes=[vm(a.shape, a.dtype) for a in shapes] + [dma((2, 12))],
    )(*held)
    return out.reshape(32, 64, 256), grad.reshape(32, 64, 256), qg, mxg


def solution(mesh):
    whole = P()
    tile = P("row", "col", None)
    return jax.shard_map(
        body,
        mesh=mesh,
        in_specs=(tile, tile) + (whole,) * 11,
        out_specs=(tile, tile, whole, whole),
        check_vma=False,
    )
```
